128 devices in a mesh: sx: 16 (over z, y), sy: 8 (over x, core).
Axes of the slice: x: 4, y: 4, z: 4, core: 2. Of those that a mesh axis runs over, the one named last changes fastest.
Arguments:
- control: float32 [2, 127, 256, 1024], P(None, None, 'sx', 'sy'), may hold values from -6 to 6
- deviation: float32 [2, 127, 256, 1024], P(None, None, 'sx', 'sy'), may hold values from 0.3 to 3
- vertical: float32 [2, 127, 127], replicated, may hold values from -0.5 to 0.5
- length: float32 [2, 127], replicated, may hold values from 1.5 to 6
- owners: int32 [254, 1], replicated, may hold values from 0 to 127; in each aligned block of 254 rows (0 to 253, 254 to 507, ...) at most 4 rows name the same one
Outputs:
- result: float32 [2, 127, 256, 1024], P(None, None, 'sx', 'sy')
- slab_fields: float32 [128, 4, 256, 1024], P(('sx', 'sy'))
The draws below stay inside these ranges and needn't reach their ends.
Inputs may be any that keep to these rules, and one draw needn't show every extreme that they name: `owners`: each device owns at most 4 slabs and some device owns exactly 4.
All inputs are finite; a program needn't handle non-finite values.
Results may differ from the reference program's by a relative error of at most 0.000071.
Values sent between devices are 32-bit elements; how exact they have to be, the bound alone decides.
A program may use at most 320 MiB of HBM per device.

```python
import math
import jax
import jax.numpy as jnp
import numpy as np
from jax import lax

VARS = 2
LEV = 127
BAND = 12
NLON = 256
NLAT = 1024
SLABS = 254
MOST = 4
DEVICES = 128


def steps_of(stream_key, shape, cuts, smallest, top_value):
    factor_of = 1.0
    for axis_at, blocks in cuts:
        steps = jax.random.uniform(jax.random.fold_in(jax.random.fold_in(stream_key, 6), axis_at), (blocks,), jnp.float32, smallest / len(cuts), top_value / len(cuts))
        factor_of = factor_of * jnp.repeat(jnp.exp(steps), shape[axis_at] // blocks).reshape((-1,) + (1,) * (len(shape) - 1 - axis_at))
    return factor_of


def shared_out(own_key, own, number, rows, amount, top, bound, skew):
    ranking = jax.random.permutation(own_key, amount)
    crowded, usual = load_shares(amount, rows * top, bound, skew, True), load_shares(amount, rows * top, bound, skew, False)
    places = jnp.arange(amount)

    def named(tallies, offset_by):
        used = int((tallies > 0).sum())
        fixed = max(1, used // 4)
        passed = fixed + (places - fixed + offset_by * (used - fixed)) % max(1, amount - fixed)
        return jnp.zeros((amount,), jnp.int32).at[ranking[jnp.where(places < fixed, places, passed)]].set(jnp.asarray(tallies, jnp.int32))

    tallies = jnp.where(number % 4 == 0, named(crowded, number // 4), named(usual, number - number // 4 - 1))
    mixed = jax.random.permutation(jax.random.fold_in(own, 3), amount)
    donor, sink = mixed[0:amount // 2 * 2:2], mixed[1:amount // 2 * 2:2]
    margin = jnp.minimum(tallies[donor] - 1, bound - tallies[sink]) // 2
    margin = jnp.where((donor == ranking[0]) | (sink == ranking[0]) | (tallies[sink] == 0), 0, jnp.maximum(margin, 0))
    passed = jax.random.randint(jax.random.fold_in(own, 4), (amount // 2,), 0, 1 << 20) % (margin + 1)
    tallies = tallies.at[donor].add(-passed).at[sink].add(passed)
    items = jnp.searchsorted(jnp.cumsum(tallies), jnp.arange(rows * top), side="right").astype(jnp.int32)
    grid = items.reshape(top, rows).T
    grid = grid[jax.random.permutation(jax.random.fold_in(own, 1), rows)]
    offset_by = jax.random.randint(jax.random.fold_in(own, 2), (rows, 1), 0, top)
    return jnp.take_along_axis(grid, (jnp.arange(top)[None, :] + offset_by) % top, axis=1)


def load_shares(number_of, total, bound, slope, full):
    weights = [(1 << 20) // math.isqrt(rank ** slope) + 1 for rank in range(1, number_of + 1)]
    largest = bound if full else min(bound, max(-(-total // number_of), total * weights[0] // sum(weights)))
    least = 1 if total - largest >= number_of - 1 else 0
    given, surplus = [largest] + [least] * (number_of - 1), total - largest - least * (number_of - 1)
    while surplus > 0:
        free = [i for i in range(1, number_of) if given[i] < largest] or [i for i in range(1, number_of) if given[i] < bound]
        whole, remaining = sum([weights[i] for i in free]), surplus
        for i in free:
            addition = min(bound - given[i], max(1, remaining * weights[i] // whole), surplus)
            given[i] = given[i] + addition
            surplus = surplus - addition
    return np.array(given)


def bell_draw(stream_key, shape, width, most, shards=(), dtype=jnp.bfloat16):
    drawn = jax.random.normal(stream_key, shape, jnp.float32) * width
    if len(shards) > 0:
        drawn = steps_of(stream_key, shape, shards, -0.22, 0.18) * drawn
    return jnp.clip(drawn, min=-most, max=most).astype(dtype)


def setup_inputs(seed: int = 0) -> dict:
    key_of = jax.random.split(jax.random.key(seed), 6)
    control = bell_draw(key_of[0], (VARS, LEV, NLON, NLAT), 1.0, 6.0, ((2, 16), (3, 8)), jnp.float32)
    deviation = jnp.clip(jnp.exp(math.log(3.0) - 2.3025851 * jax.random.uniform(key_of[1], (VARS, LEV, NLON, NLAT), jnp.float32) ** steps_of(key_of[1], (VARS, LEV, NLON, NLAT), ((2, 16), (3, 8)), -0.2, 0.2)), 0.3, 3.0)
    vertical = bell_draw(key_of[2], (VARS, LEV, LEV), LEV ** -0.5, 0.5, (), jnp.float32)
    length = jnp.clip(jnp.exp(jax.random.uniform(key_of[3], (VARS, LEV), jnp.float32, math.log(1.5), math.log(6.0))), 1.5, 6.0)
    owners_keys = jax.random.split(jax.random.fold_in(key_of[4], 1), SLABS // SLABS)
    owners_turns = jax.random.permutation(jax.random.fold_in(key_of[4], 3), SLABS // SLABS)
    owners = jax.vmap(lambda own, number: shared_out(jax.random.fold_in(key_of[4], 2), own, number, SLABS, DEVICES, 1, MOST, 2))(owners_keys, owners_turns).reshape((SLABS, 1))
    return dict(control=control, deviation=deviation, vertical=vertical, length=length, owners=owners)


def band_weights(scales):
    offsets = jnp.arange(-BAND, BAND + 1).astype(jnp.float32)
    bell = jnp.exp(-(offsets[None, :] * offsets[None, :]) / (2.0 * scales[:, None] * scales[:, None]))
    return bell / jnp.sqrt(lax.optimization_barrier(jnp.sum(bell * bell, axis=1, keepdims=True)))

def slab_slots(owners_flat):
    positions = jnp.arange(owners_flat.shape[0]).astype(jnp.int32)
    earlier = (owners_flat[:, None] == owners_flat[None, :]) & (positions[None, :] < positions[:, None])
    return lax.optimization_barrier(jnp.sum(earlier.astype(jnp.int32), axis=1)).astype(jnp.int32)

def smooth_one(pieces):
    plane, weights = pieces
    along_lon = jnp.zeros_like(plane)
    for shift_index in range(2 * BAND + 1):
        along_lon = along_lon + weights[shift_index] * jnp.roll(plane, BAND - shift_index, axis=0)
    padded = jnp.pad(along_lon, ((0, 0), (BAND, BAND)))
    along_lat = jnp.zeros_like(plane)
    for shift_index in range(2 * BAND + 1):
        along_lat = along_lat + weights[shift_index] * padded[:, shift_index:shift_index + plane.shape[1]]
    return along_lat

def reference(control, deviation, vertical, length, owners):
    count = VARS * LEV
    scaled = deviation * control
    lifted = jnp.einsum('vkj,vjab->vkab', vertical, scaled, precision=lax.Precision.HIGHEST)
    weights = band_weights(length.reshape(count))
    smoothed = lax.map(smooth_one, (lifted.reshape(count, NLON, NLAT), weights))
    owners_flat = owners.reshape(count).astype(jnp.int32)
    slots = slab_slots(owners_flat)
    slab_fields = jnp.zeros((DEVICES, MOST, NLON, NLAT), jnp.float32).at[owners_flat, slots].set(smoothed)
    settled = jnp.einsum('vkj,vkab->vjab', vertical, smoothed.reshape(VARS, LEV, NLON, NLAT), precision=lax.Precision.HIGHEST)
    return (deviation * settled, slab_fields)
```

```python
import functools

import jax
import jax.numpy as jnp
from jax import lax
from jax.experimental import pallas as pl
from jax.experimental.pallas import tpu as pltpu
from jax.sharding import PartitionSpec as P

MESH = pl.DeviceIdType.MESH
BAND = 12
VARS, LEV, ROWS, COLS = 2, 127, 16, 128
SX, SY = 16, 8
DEVICES = SX * SY
NLON, NLAT = 256, 1024
PLACES = 2 * DEVICES
LIFT = VARS * LEV * ROWS
VMEM_LIMIT = 56 * 2**20


def split(x):
    high = x.astype(jnp.bfloat16)
    return high, (x - high.astype(jnp.float32)).astype(jnp.bfloat16)


def dot(a, b):
    return jnp.dot(a, b, preferred_element_type=jnp.float32)


def dot3(a, b):
    return dot(a[0], b[0]) + (dot(a[0], b[1]) + dot(a[1], b[0]))


def where_to(owner_col, owner_row):
    shape = (PLACES, PLACES)
    down = lax.broadcasted_iota(jnp.int32, shape, 0).astype(jnp.float32)
    over = lax.broadcasted_iota(jnp.int32, shape, 1).astype(jnp.float32)
    one = lambda c: jnp.where(c, 1.0, 0.0)
    same = one(owner_col == owner_row)
    below, above = one(over < down), one(down < over)
    slot_row = jnp.sum(same * above, axis=0, keepdims=True)
    slot_col = jnp.sum(same * below, axis=1, keepdims=True)
    real_row, real_col = one(owner_row >= 0.0), one(owner_col >= 0.0)
    extra_row = real_row * one(slot_row >= 2.0)
    extra_col = real_col * one(slot_col >= 2.0)
    native_row = jnp.where(real_row * (1.0 - extra_row) > 0.0, 2.0 * owner_row + slot_row, -1.0)
    native_col = jnp.where(real_col * (1.0 - extra_col) > 0.0, 2.0 * owner_col + slot_col, -1.0)
    native = one(down == native_row)
    taken_col = jnp.sum(native, axis=1, keepdims=True)
    taken_row = jnp.sum(one(native_col == over), axis=0, keepdims=True)
    rank_row = jnp.sum(extra_col * above, axis=0, keepdims=True)
    free_rank_col = jnp.sum((1.0 - taken_row) * below, axis=1, keepdims=True)
    lent = one(free_rank_col == rank_row) * extra_row * (1.0 - taken_col)
    extra = one(down == 2.0 * owner_row + slot_row - 2.0) * extra_row
    return native + lent, extra, taken_col


def lift_kernel(
    control_hbm, deviation_hbm, vertical_ref, length_ref, owners_ref,
    pieces_hbm, back_high_ref, back_low_ref, facts_ref,
    control, deviation, pieces, matrix, owner_ref, length_row_ref, in_sem, out_sem,
):
    me = (lax.axis_index("sx") * SY + lax.axis_index("sy")).astype(jnp.float32)
    cut = LIFT // 2
    loads = []
    for part in range(2):
        rows = pl.ds(part * cut, cut)
        for at, (src, dst) in enumerate(((control_hbm, control), (deviation_hbm, deviation))):
            loads.append(pltpu.make_async_copy(src.at[rows], dst.at[rows], in_sem.at[2 * part + at]))
    for load in loads:
        load.start()
    control[LIFT:, :] = jnp.zeros((ROWS, COLS), jnp.float32)
    deviation[LIFT:, :] = jnp.zeros((ROWS, COLS), jnp.float32)

    owner_ref[...] = jnp.full((PLACES, 1), -1, jnp.int32)
    length_row_ref[...] = jnp.ones((1, PLACES), jnp.float32)
    matrix[...] = jnp.zeros((PLACES, PLACES), jnp.float32)
    for v in range(VARS):
        owner_ref[v * 128 : v * 128 + LEV, :] = owners_ref[v * LEV : (v + 1) * LEV, :]
        length_row_ref[:, v * 128 : v * 128 + LEV] = length_ref[v : v + 1, :]
        matrix[v * 128 : v * 128 + LEV, v * 128 : v * 128 + LEV] = vertical_ref[v]
    owner_col = owner_ref[...].astype(jnp.float32)
    shape = (PLACES, PLACES)
    down = lax.broadcasted_iota(jnp.int32, shape, 0)
    over = lax.broadcasted_iota(jnp.int32, shape, 1)
    owner_row = jnp.sum(jnp.where(down == over, owner_col, 0.0), axis=0, keepdims=True)
    home, extra, taken_col = where_to(owner_col, owner_row)

    length_row = length_row_ref[...]
    place = lax.broadcasted_iota(jnp.int32, (PLACES, 1), 0).astype(jnp.float32)
    for at, hot in ((0, home), (2, extra)):
        used = jnp.sum(hot, axis=1, keepdims=True)
        long = jnp.sum(hot * length_row, axis=1, keepdims=True) + (1.0 - used)
        for h in range(2):
            mine = jnp.where(place == 2.0 * me + h, 1.0, 0.0)
            facts_ref[at + h : at + h + 1, :] = jnp.broadcast_to(jnp.sum(mine * long, axis=0, keepdims=True), (1, COLS))
            if at == 0:
                facts_ref[4 + h : 5 + h, :] = jnp.broadcast_to(jnp.sum(mine * taken_col, axis=0, keepdims=True), (1, COLS))
    facts_ref[6:8, :] = jnp.zeros((2, COLS), jnp.float32)

    high, low = split(matrix[...])
    hots = jnp.concatenate([home, extra], axis=0).astype(jnp.bfloat16)
    rows_high = dot(hots, high).astype(jnp.bfloat16)
    rows_low = dot(hots, low).astype(jnp.bfloat16)
    turned_high, turned_low = split(matrix[...].T)
    home_turned = home.T.astype(jnp.bfloat16)
    back_high_ref[...] = dot(turned_high, home_turned).astype(jnp.bfloat16)
    back_low_ref[...] = dot(turned_low, home_turned).astype(jnp.bfloat16)

    for load in loads:
        load.wait()
    for i in range(0, ROWS, 2):
        sides = []
        for r in (i, i + 1):
            halves = []
            for v in range(VARS):
                at = pl.ds(v * LEV * ROWS + r, 128, stride=ROWS)
                halves.append(control[at, :] * deviation[at, :])
            sides.append(jnp.concatenate(halves, axis=0))
        lifted = dot3((rows_high, rows_low), split(jnp.concatenate(sides, axis=1)))
        for r in (0, 1):
            pieces[pl.ds(i + r, 2 * PLACES, stride=ROWS), :] = lifted[:, r * COLS : (r + 1) * COLS]
    out = pltpu.make_async_copy(pieces, pieces_hbm, out_sem)
    out.start()
    out.wait()


def smooth_matrices(long, lon, lat):
    lane = lax.broadcasted_iota(jnp.int32, (8, COLS), 1)
    offset = (lane - BAND).astype(jnp.float32)
    bell = jnp.where(lane <= 2 * BAND, jnp.exp(-(offset * offset) / (2.0 * long * long)), 0.0)
    norm = jnp.sqrt(jnp.sum(bell * bell, axis=1, keepdims=True))[0:1, :]

    def weigh(d):
        near = (d >= -BAND) & (d <= BAND)
        d = d.astype(jnp.float32)
        return jnp.where(near, jnp.exp(-(d * d) / (2.0 * long[:, :1] * long[:, :1])) / norm, 0.0)

    shape = (NLON, NLON)
    d = lax.broadcasted_iota(jnp.int32, shape, 1) - lax.broadcasted_iota(jnp.int32, shape, 0)
    d = jnp.where(d >= NLON // 2, d - NLON, jnp.where(d < -(NLON // 2), d + NLON, d))
    lon[0], lon[1] = split(weigh(d))
    shape = (512, 256)
    d = lax.broadcasted_iota(jnp.int32, shape, 0) - 128 - lax.broadcasted_iota(jnp.int32, shape, 1)
    lat[0], lat[1] = split(weigh(d))


def travel_kernel(
    pieces, facts, returned, slabs,
    home, extra, outgoing, field, along, lon, lat,
    send_sem, home_sem, extra_sem, back_sem, own_sem, field_sem,
):
    mx, my = lax.axis_index("sx"), lax.axis_index("sy")
    me = mx * SY + my
    z, y, x, core = mx // 4, mx % 4, my // 2, my % 2

    def partner(step):
        k = DEVICES - step
        px = ((z + (k // 4) % 4) % 4) * 4 + (y + (k // 16) % 4) % 4
        py = ((x + k % 4) % 4) * 2 + (core + k // 64) % 2
        return px, py

    barrier = pltpu.get_barrier_semaphore()

    @pl.loop(1, DEVICES)
    def _(step):
        px, py = partner(step)
        pl.semaphore_signal(barrier, inc=1, device_id=(px, py), device_id_type=MESH)

    for h in range(2):
        smooth_matrices(facts[h : h + 1, :], lon.at[h], lat.at[h])
    here = my * SX + mx
    own_home = pltpu.make_async_copy(pieces.at[pl.ds(2 * me, 2)], home.at[here], own_sem.at[0])
    own_extra = pltpu.make_async_copy(pieces.at[pl.ds(PLACES + 2 * me, 2)], extra.at[here], own_sem.at[1])
    own_home.start()
    own_extra.start()
    pl.semaphore_wait(barrier, DEVICES - 1)

    def scatter(first, into, sem):
        @pl.loop(1, DEVICES)
        def _(step):
            px, py = partner(step)
            pltpu.make_async_remote_copy(
                src_ref=pieces.at[pl.ds(first + 2 * (px * SY + py), 2)],
                dst_ref=into.at[here],
                send_sem=send_sem,
                recv_sem=sem,
                device_id=(px, py),
                device_id_type=MESH,
            ).start()

    scatter(0, home, home_sem)
    scatter(PLACES, extra, extra_sem)

    def smooth(h, source, keep):
        for t in range(4):
            blocks = [source[pl.ds((2 * t + b) * SX, SX), h].reshape(NLON, COLS) for b in range(2)]
            lifted = split(jnp.concatenate(blocks, axis=1))
            along[:, t * 256 : (t + 1) * 256] = dot3((lon[h, 0], lon[h, 1]), lifted)
        for t in range(4):
            begin, end = max(0, 256 * t - 128), min(NLAT, 256 * t + 384)
            skip = begin - (256 * t - 128)
            taps = pl.ds(skip, end - begin)
            done = dot3(split(along[:, begin:end]), (lat[h, 0, taps, :], lat[h, 1, taps, :]))
            field[keep, :, t * 256 : (t + 1) * 256] = done

    own_home.wait()
    pltpu.make_async_copy(home.at[pl.ds(0, DEVICES - 1)], home.at[pl.ds(0, DEVICES - 1)], home_sem).wait()
    for h in range(2):
        smooth(h, home, h)
        for b in range(SY):
            outgoing[pl.ds(b * SX, SX), h] = field[h, :, b * COLS : (b + 1) * COLS].reshape(SX, ROWS, COLS)

    own_back = pltpu.make_async_copy(outgoing.at[here], returned.at[pl.ds(2 * me, 2)], own_sem.at[2])
    own_back.start()

    @pl.loop(1, DEVICES)
    def _(step):
        px, py = partner(step)
        pltpu.make_async_remote_copy(
            src_ref=outgoing.at[py * SX + px],
            dst_ref=returned.at[pl.ds(2 * me, 2)],
            send_sem=send_sem,
            recv_sem=back_sem,
            device_id=(px, py),
            device_id_type=MESH,
        ).start()

    for h in range(2):
        field[h] = field[h] * facts[4 + h : 5 + h, :1]
    out = [pltpu.make_async_copy(field.at[pl.ds(0, 2)], slabs.at[pl.ds(0, 2)], field_sem.at[0])]
    out[0].start()
    for h in range(2):
        smooth_matrices(facts[2 + h : 3 + h, :], lon.at[h], lat.at[h])
    own_extra.wait()
    pltpu.make_async_copy(extra.at[pl.ds(0, DEVICES - 1)], extra.at[pl.ds(0, DEVICES - 1)], extra_sem).wait()
    for h in range(2):
        smooth(h, extra, 2 + h)
        out.append(pltpu.make_async_copy(field.at[2 + h], slabs.at[2 + h], field_sem.at[1 + h]))
        out[-1].start()
    own_back.wait()
    for copy in out:
        copy.wait()
    arrived = returned.at[pl.ds(0, 2 * (DEVICES - 1))]
    pltpu.make_async_copy(arrived, arrived, back_sem).wait()
    for _ in range(3):
        pltpu.make_async_copy(arrived, arrived, send_sem).wait()


def settle_kernel(
    returned_hbm, deviation_hbm, back_high, back_low, slabs_hbm,
    result_hbm, fields_hbm,
    returned, deviation, result, fields, in_sem, out_sem,
):
    loads = [
        pltpu.make_async_copy(returned_hbm, returned, in_sem.at[0]),
        pltpu.make_async_copy(deviation_hbm, deviation, in_sem.at[1]),
    ]
    slots = [pltpu.make_async_copy(slabs_hbm.at[h], fields.at[h], in_sem.at[2 + h]) for h in range(4)]
    for load in loads + slots:
        load.start()
    for load in loads:
        load.wait()
    back = (back_high[...], back_low[...])
    for i in range(0, ROWS, 2):
        sides = [returned[pl.ds(i + r, PLACES, stride=ROWS), :] for r in range(2)]
        settled = dot3(back, split(jnp.concatenate(sides, axis=1)))
        for r in range(2):
            for v in range(VARS):
                at = pl.ds(v * LEV * ROWS + i + r, LEV, stride=ROWS)
                result[at, :] = deviation[at, :] * settled[v * 128 : v * 128 + LEV, r * COLS : (r + 1) * COLS]
        if i == 0:
            out = []
            for h in range(4):
                slots[h].wait()
                out.append(pltpu.make_async_copy(fields.at[h], fields_hbm.at[h], out_sem.at[h]))
                out[h].start()
    half = LIFT // 2
    for part in range(2):
        rows = pl.ds(part * half, half)
        out.append(pltpu.make_async_copy(result.at[rows], result_hbm.at[rows], out_sem.at[4 + part]))
        out[-1].start()
    for copy in out:
        copy.wait()


def local(control, deviation, vertical, length, owners):
    f32, bf16 = jnp.float32, jnp.bfloat16
    vmem, hbm = pl.BlockSpec(memory_space=pltpu.VMEM), pl.BlockSpec(memory_space=pl.ANY)
    dma = pltpu.SemaphoreType.DMA
    flat = (LIFT, COLS)
    deviation = deviation.reshape(flat)
    pieces, back_high, back_low, facts = pl.pallas_call(
        lift_kernel,
        out_shape=[
            jax.ShapeDtypeStruct((2 * PLACES * ROWS, COLS), f32),
            jax.ShapeDtypeStruct((PLACES, PLACES), bf16),
            jax.ShapeDtypeStruct((PLACES, PLACES), bf16),
            jax.ShapeDtypeStruct((8, COLS), f32),
        ],
        in_specs=[hbm, hbm, vmem, vmem, vmem],
        out_specs=[hbm, vmem, vmem, vmem],
        scratch_shapes=[
            pltpu.VMEM((LIFT + ROWS, COLS), f32),
            pltpu.VMEM((LIFT + ROWS, COLS), f32),
            pltpu.VMEM((2 * PLACES * ROWS, COLS), f32),
            pltpu.VMEM((PLACES, PLACES), f32),
            pltpu.VMEM((PLACES, 1), jnp.int32),
            pltpu.VMEM((1, PLACES), f32),
            dma((4,)),
            dma,
        ],
        compiler_params=pltpu.CompilerParams(vmem_limit_bytes=VMEM_LIMIT),
        name="lift",
    )(control.reshape(flat), deviation, vertical, length, owners)

    block = (DEVICES, 2, ROWS, COLS)
    returned, slabs = pl.pallas_call(
        travel_kernel,
        out_shape=[
            jax.ShapeDtypeStruct((PLACES, ROWS, COLS), f32),
            jax.ShapeDtypeStruct((4, NLON, NLAT), f32),
        ],
        in_specs=[hbm, vmem],
        out_specs=[hbm, hbm],
        scratch_shapes=[
            pltpu.VMEM(block, f32),
            pltpu.VMEM(block, f32),
            pltpu.VMEM(block, f32),
            pltpu.VMEM((4, NLON, NLAT), f32),
            pltpu.VMEM((NLON, NLAT), f32),
            pltpu.VMEM((2, 2, NLON, NLON), bf16),
            pltpu.VMEM((2, 2, 512, 256), bf16),
            dma, dma, dma, dma, dma((3,)), dma((3,)),
        ],
        compiler_params=pltpu.CompilerParams(
            collective_id=0, has_side_effects=True, vmem_limit_bytes=VMEM_LIMIT
        ),
        name="travel",
    )(pieces.reshape(2 * PLACES, ROWS, COLS), facts)

    result, fields = pl.pallas_call(
        settle_kernel,
        out_shape=[
            jax.ShapeDtypeStruct(flat, f32),
            jax.ShapeDtypeStruct((4, NLON, NLAT), f32),
        ],
        in_specs=[hbm, hbm, vmem, vmem, hbm],
        out_specs=[hbm, hbm],
        scratch_shapes=[
            pltpu.VMEM((PLACES * ROWS, COLS), f32),
            pltpu.VMEM(flat, f32),
            pltpu.VMEM(flat, f32),
            pltpu.VMEM((4, NLON, NLAT), f32),
            dma((6,)),
            dma((6,)),
        ],
        compiler_params=pltpu.CompilerParams(vmem_limit_bytes=VMEM_LIMIT),
        name="settle",
    )(returned.reshape(PLACES * ROWS, COLS), deviation, back_high, back_low, slabs)
    return result.reshape(VARS, LEV, ROWS, COLS), fields.reshape(1, 4, NLON, NLAT)


def solution(mesh):
    return jax.shard_map(
        local,
        mesh=mesh,
        in_specs=(P(None, None, "sx", "sy"), P(None, None, "sx", "sy"), P(), P(), P()),
        out_specs=(P(None, None, "sx", "sy"), P(("sx", "sy"), None, None, None)),
        check_vma=False,
    )
```

```python
import jax
import jax.numpy as jnp
from jax import lax
from jax.experimental import pallas as pl
from jax.experimental.pallas import tpu as pltpu
from jax.sharding import PartitionSpec as P

MESH = pl.DeviceIdType.MESH
BAND = 12
VARS, LEV, ROWS, COLS = 2, 127, 16, 128
SX, SY = 16, 8
DEVICES = SX * SY
VMEM_LIMIT = 57 * 2**20
NLON, NLAT = 256, 1024
PLACES = 2 * DEVICES
LIFT = VARS * LEV * ROWS


def split(x):
    high = x.astype(jnp.bfloat16)
    return high, (x - high.astype(jnp.float32)).astype(jnp.bfloat16)


def dot(a, b):
    return jnp.dot(a, b, preferred_element_type=jnp.float32)


def dot3(a, b):
    return dot(a[0], b[0]) + (dot(a[0], b[1]) + dot(a[1], b[0]))


def where_to(owner_col, owner_row):
    shape = (PLACES, PLACES)
    down = lax.broadcasted_iota(jnp.int32, shape, 0).astype(jnp.float32)
    over = lax.broadcasted_iota(jnp.int32, shape, 1).astype(jnp.float32)
    one = lambda c: jnp.where(c, 1.0, 0.0)
    same = one(owner_col == owner_row)
    below, above = one(over < down), one(down < over)
    slot_row = jnp.sum(same * above, axis=0, keepdims=True)
    slot_col = jnp.sum(same * below, axis=1, keepdims=True)
    real_row, real_col = one(owner_row >= 0.0), one(owner_col >= 0.0)
    extra_row = real_row * one(slot_row >= 2.0)
    extra_col = real_col * one(slot_col >= 2.0)
    native_row = jnp.where(real_row * (1.0 - extra_row) > 0.0, 2.0 * owner_row + slot_row, -1.0)
    native_col = jnp.where(real_col * (1.0 - extra_col) > 0.0, 2.0 * owner_col + slot_col, -1.0)
    native = one(down == native_row)
    taken_col = jnp.sum(native, axis=1, keepdims=True)
    taken_row = jnp.sum(one(native_col == over), axis=0, keepdims=True)
    rank_row = jnp.sum(extra_col * above, axis=0, keepdims=True)
    free_rank_col = jnp.sum((1.0 - taken_row) * below, axis=1, keepdims=True)
    lent = one(free_rank_col == rank_row) * extra_row * (1.0 - taken_col)
    extra = one(down == 2.0 * owner_row + slot_row - 2.0) * extra_row
    return native + lent, extra, taken_col


def smooth_matrices(long, lon, lat):
    lane = lax.broadcasted_iota(jnp.int32, (8, COLS), 1)
    offset = (lane - BAND).astype(jnp.float32)
    bell = jnp.where(lane <= 2 * BAND, jnp.exp(-(offset * offset) / (2.0 * long * long)), 0.0)
    norm = jnp.sqrt(jnp.sum(bell * bell, axis=1, keepdims=True))[0:1, :]

    def weigh(d):
        near = (d >= -BAND) & (d <= BAND)
        d = d.astype(jnp.float32)
        return jnp.where(near, jnp.exp(-(d * d) / (2.0 * long * long)) / norm, 0.0)

    shape = (NLON, NLON)
    d = lax.broadcasted_iota(jnp.int32, shape, 1) - lax.broadcasted_iota(jnp.int32, shape, 0)
    d = jnp.where(d >= NLON // 2, d - NLON, jnp.where(d < -(NLON // 2), d + NLON, d))
    lon[0], lon[1] = split(weigh(d))
    shape = (512, 256)
    d = lax.broadcasted_iota(jnp.int32, shape, 0) - 128 - lax.broadcasted_iota(jnp.int32, shape, 1)
    lat[0], lat[1] = split(weigh(d))


def travel_kernel(
    control_hbm, deviation_hbm, vertical_hbm, length_hbm, owners_hbm,
    returned, field_hbm, back_hbm,
    control, deviation, vertical_ref, length_ref, owners_ref, scaled, pieces, matrix, length_row_ref,
    home, extra, outgoing, along, lon, lat, field, back,
    in_sem, send_sem, home_sem, extra_sem, back_sem, own_sem, out_sem,
):
    mx, my = lax.axis_index("sx"), lax.axis_index("sy")
    me = mx * SY + my
    here = my * SX + mx
    z, y, x, core = mx // 4, mx % 4, my // 2, my % 2

    def partner(step):
        k = DEVICES - step
        px = ((z + (k // 4) % 4) % 4) * 4 + (y + (k // 16) % 4) % 4
        py = ((x + k % 4) % 4) * 2 + (core + k // 64) % 2
        return px, py

    cut = LIFT // 2
    small = []
    for at, (src, dst) in enumerate(
        ((owners_hbm, owners_ref), (vertical_hbm, vertical_ref), (length_hbm, length_ref))
    ):
        small.append(pltpu.make_async_copy(src, dst, in_sem.at[4 + at]))
        small[-1].start()
    loads = []
    for part in range(2):
        rows = pl.ds(part * cut, cut)
        for at, (src, dst) in enumerate(((control_hbm, control), (deviation_hbm, deviation))):
            loads.append(pltpu.make_async_copy(src.at[rows], dst.at[rows], in_sem.at[2 * part + at]))
    for load in loads:
        load.start()

    barrier = pltpu.get_barrier_semaphore()

    @pl.loop(1, DEVICES)
    def _(step):
        px, py = partner(step)
        pl.semaphore_signal(barrier, inc=1, device_id=(px, py), device_id_type=MESH)

    control[LIFT:, :] = jnp.zeros((ROWS, COLS), jnp.float32)
    deviation[LIFT:, :] = jnp.zeros((ROWS, COLS), jnp.float32)
    length_row_ref[...] = jnp.ones((1, PLACES), jnp.float32)
    matrix[...] = jnp.zeros((PLACES, PLACES), jnp.float32)
    for load in small:
        load.wait()
    for v in range(VARS):
        length_row_ref[:, v * 128 : v * 128 + LEV] = length_ref[v : v + 1, :]
        matrix[v * 128 : v * 128 + LEV, v * 128 : v * 128 + LEV] = vertical_ref[:, v, :]
    slab = lax.broadcasted_iota(jnp.int32, (PLACES, VARS * LEV), 0)
    level = slab % 128
    number = jnp.where(level < LEV, slab - slab // 128, -1)
    listed = lax.broadcasted_iota(jnp.int32, (PLACES, VARS * LEV), 1) == number
    owners = owners_ref[...].astype(jnp.float32)
    owner_col = jnp.sum(jnp.where(listed, owners + 1.0, 0.0), axis=1, keepdims=True) - 1.0
    shape = (PLACES, PLACES)
    down = lax.broadcasted_iota(jnp.int32, shape, 0)
    over = lax.broadcasted_iota(jnp.int32, shape, 1)
    owner_row = jnp.sum(jnp.where(down == over, owner_col, 0.0), axis=0, keepdims=True)
    home_hot, extra_hot, taken_col = where_to(owner_col, owner_row)
    high, low = split(matrix[...])

    def lift(hot, first):
        hot = hot.astype(jnp.bfloat16)
        rows = (dot(hot, high).astype(jnp.bfloat16), dot(hot, low).astype(jnp.bfloat16))
        for i in range(0, ROWS, 2):
            lifted = dot3(rows, (scaled[0, i // 2], scaled[1, i // 2]))
            for r in (0, 1):
                at = pl.ds(first * ROWS + i + r, PLACES, stride=ROWS)
                pieces[at, :] = lifted[:, r * COLS : (r + 1) * COLS]

    def two(first, device):
        return pieces.at[pl.ds((first + 2 * device) * ROWS, 2 * ROWS)]

    def scatter(first, into, sem):
        @pl.loop(1, DEVICES)
        def _(step):
            px, py = partner(step)
            pltpu.make_async_remote_copy(
                src_ref=two(first, px * SY + py),
                dst_ref=into.at[here],
                send_sem=send_sem,
                recv_sem=sem,
                device_id=(px, py),
                device_id_type=MESH,
            ).start()

    for load in loads:
        load.wait()
    for i in range(0, ROWS, 2):
        sides = []
        for r in (i, i + 1):
            halves = []
            for v in range(VARS):
                at = pl.ds(v * LEV * ROWS + r, 128, stride=ROWS)
                halves.append(control[at, :] * deviation[at, :])
            sides.append(jnp.concatenate(halves, axis=0))
        scaled[0, i // 2], scaled[1, i // 2] = split(jnp.concatenate(sides, axis=1))

    lift(home_hot, 0)
    pl.semaphore_wait(barrier, DEVICES - 1)
    scatter(0, home, home_sem)
    own_home = pltpu.make_async_copy(two(0, me), home.at[here], own_sem.at[0])
    own_home.start()
    lift(extra_hot, PLACES)
    scatter(PLACES, extra, extra_sem)
    own_extra = pltpu.make_async_copy(two(PLACES, me), extra.at[here], own_sem.at[1])
    own_extra.start()

    turned_high, turned_low = split(matrix[...].T)
    home_turned = home_hot.T.astype(jnp.bfloat16)
    back[0] = dot(turned_high, home_turned).astype(jnp.bfloat16)
    back[1] = dot(turned_low, home_turned).astype(jnp.bfloat16)
    out = [pltpu.make_async_copy(back, back_hbm, out_sem.at[4])]
    out[0].start()
    length_row = length_row_ref[...]
    place = lax.broadcasted_iota(jnp.int32, (PLACES, 1), 0).astype(jnp.float32)
    owned = []
    for at, hot in ((0, home_hot), (2, extra_hot)):
        used = jnp.sum(hot, axis=1, keepdims=True)
        long = jnp.sum(hot * length_row, axis=1, keepdims=True) + (1.0 - used)
        for h in range(2):
            mine = jnp.where(place == (2 * me + h).astype(jnp.float32), 1.0, 0.0)
            smooth_matrices(jnp.sum(mine * long, axis=0, keepdims=True), lon.at[at + h], lat.at[at + h])
            if at == 0:
                owned.append(jnp.sum(mine * taken_col, axis=0, keepdims=True))

    def smooth(h, source, keep):
        for t in range(4):
            blocks = [
                source[pl.ds((2 * t + b) * SX, SX), h * ROWS : (h + 1) * ROWS].reshape(NLON, COLS) for b in range(2)
            ]
            lifted = split(jnp.concatenate(blocks, axis=1))
            along[:, t * 256 : (t + 1) * 256] = dot3((lon[keep, 0], lon[keep, 1]), lifted)
        for t in range(4):
            begin, end = max(0, 256 * t - 128), min(NLAT, 256 * t + 384)
            taps = pl.ds(begin - (256 * t - 128), end - begin)
            done = dot3(split(along[:, begin:end]), (lat[keep, 0, taps, :], lat[keep, 1, taps, :]))
            if keep < 2:
                field[keep, :, t * 256 : (t + 1) * 256] = done * owned[keep]
                for b in range(2):
                    outgoing[pl.ds((2 * t + b) * SX, SX), h * ROWS : (h + 1) * ROWS] = done[
                        :, b * COLS : (b + 1) * COLS
                    ].reshape(SX, ROWS, COLS)
            else:
                field[keep, :, t * 256 : (t + 1) * 256] = done

    own_home.wait()
    pltpu.make_async_copy(home.at[pl.ds(0, DEVICES - 1)], home.at[pl.ds(0, DEVICES - 1)], home_sem).wait()
    for h in range(2):
        smooth(h, home, h)
    into = returned.at[pl.ds(2 * ROWS * me, 2 * ROWS)]
    own_back = pltpu.make_async_copy(outgoing.at[here], into, own_sem.at[2])
    own_back.start()

    @pl.loop(1, DEVICES)
    def _(step):
        px, py = partner(step)
        pltpu.make_async_remote_copy(
            src_ref=outgoing.at[py * SX + px],
            dst_ref=into,
            send_sem=send_sem,
            recv_sem=back_sem,
            device_id=(px, py),
            device_id_type=MESH,
        ).start()

    def write(h):
        out.append(pltpu.make_async_copy(field.at[h], field_hbm.at[h], out_sem.at[h]))
        out[-1].start()

    for h in range(2):
        write(h)
    own_extra.wait()
    pltpu.make_async_copy(extra.at[pl.ds(0, DEVICES - 1)], extra.at[pl.ds(0, DEVICES - 1)], extra_sem).wait()
    for h in range(2):
        smooth(h, extra, 2 + h)
        write(2 + h)
    own_back.wait()
    for copy in out:
        copy.wait()
    arrived = returned.at[pl.ds(0, 2 * ROWS * (DEVICES - 1))]
    pltpu.make_async_copy(arrived, arrived, back_sem).wait()
    for _ in range(3):
        pltpu.make_async_copy(arrived, arrived, send_sem).wait()


def settle_kernel(
    returned_hbm, deviation_hbm, back_hbm, field_hbm,
    result_hbm, fields_hbm,
    returned, deviation, back, field, result, in_sem, out_sem,
):
    half = ROWS // 2
    loads = [pltpu.make_async_copy(back_hbm, back, in_sem.at[0])]
    for part in range(2):
        rows = pl.ds(part * half, half)
        at = 1 + 2 * part
        loads.append(pltpu.make_async_copy(returned_hbm.at[:, rows], returned.at[part], in_sem.at[at]))
        loads.append(pltpu.make_async_copy(deviation_hbm.at[:, rows], deviation.at[part], in_sem.at[at + 1]))
    slots = [pltpu.make_async_copy(field_hbm.at[h], field.at[h], in_sem.at[5 + h]) for h in range(4)]
    for load in loads + slots:
        load.start()
    out = []

    def write(src, dst):
        out.append(pltpu.make_async_copy(src, dst, out_sem.at[len(out)]))
        out[-1].start()

    loads[0].wait()
    ways = (back[0], back[1])
    for part in range(2):
        for load in loads[1 + 2 * part : 3 + 2 * part]:
            load.wait()
        arrived = returned.at[part].reshape(PLACES * half, COLS)
        spread = deviation.at[part].reshape(VARS * LEV * half, COLS)
        settled_to = result.at[part].reshape(VARS * LEV * half, COLS)
        for i in range(0, half, 2):
            sides = [arrived[pl.ds(i + r, PLACES, stride=half), :] for r in range(2)]
            settled = dot3(ways, split(jnp.concatenate(sides, axis=1)))
            for r in range(2):
                for v in range(VARS):
                    at = pl.ds(v * LEV * half + i + r, LEV, stride=half)
                    settled_to[at, :] = spread[at, :] * settled[v * 128 : v * 128 + LEV, r * COLS : (r + 1) * COLS]
            slot = part * 2 + i // 4
            if i % 4 == 0:
                slots[slot].wait()
                write(field.at[slot], fields_hbm.at[slot])
        write(result.at[part], result_hbm.at[:, pl.ds(part * half, half)])
    for copy in out:
        copy.wait()


def local(control, deviation, vertical, length, owners):
    f32, bf16 = jnp.float32, jnp.bfloat16
    hbm = pl.BlockSpec(memory_space=pl.ANY)
    dma = pltpu.SemaphoreType.DMA
    flat, square = (LIFT, COLS), (PLACES, PLACES)
    block = (DEVICES, 2 * ROWS, COLS)
    deviation = deviation.reshape(flat)
    returned, field, back = pl.pallas_call(
        travel_kernel,
        out_shape=[
            jax.ShapeDtypeStruct((PLACES * ROWS, COLS), f32),
            jax.ShapeDtypeStruct((4, NLON, NLAT), f32),
            jax.ShapeDtypeStruct((2,) + square, bf16),
        ],
        in_specs=[hbm] * 5,
        out_specs=[hbm] * 3,
        scratch_shapes=[
            pltpu.VMEM((LIFT + ROWS, COLS), f32),
            pltpu.VMEM((LIFT + ROWS, COLS), f32),
            pltpu.VMEM((LEV, VARS, LEV), f32),
            pltpu.VMEM((VARS, LEV), f32),
            pltpu.VMEM((1, VARS * LEV), jnp.int32),
            pltpu.VMEM((2, ROWS // 2, PLACES, 2 * COLS), bf16),
            pltpu.VMEM((2 * PLACES * ROWS, COLS), f32),
            pltpu.VMEM(square, f32),
            pltpu.VMEM((1, PLACES), f32),
            pltpu.VMEM(block, f32),
            pltpu.VMEM(block, f32),
            pltpu.VMEM(block, f32),
            pltpu.VMEM((NLON, NLAT), f32),
            pltpu.VMEM((4, 2, NLON, NLON), bf16),
            pltpu.VMEM((4, 2, 512, 256), bf16),
            pltpu.VMEM((4, NLON, NLAT), f32),
            pltpu.VMEM((2,) + square, bf16),
            dma((7,)), dma, dma, dma, dma, dma((3,)), dma((5,)),
        ],
        compiler_params=pltpu.CompilerParams(
            collective_id=0, has_side_effects=True, vmem_limit_bytes=VMEM_LIMIT
        ),
        name="travel",
    )(control.reshape(flat), deviation, vertical.transpose(1, 0, 2), length, owners.reshape(1, VARS * LEV))

    half = (2, VARS * LEV, ROWS // 2, COLS)
    result, fields = pl.pallas_call(
        settle_kernel,
        out_shape=[
            jax.ShapeDtypeStruct((VARS * LEV, ROWS, COLS), f32),
            jax.ShapeDtypeStruct((4, NLON, NLAT), f32),
        ],
        in_specs=[hbm] * 4,
        out_specs=[hbm] * 2,
        scratch_shapes=[
            pltpu.VMEM((2, PLACES, ROWS // 2, COLS), f32),
            pltpu.VMEM(half, f32),
            pltpu.VMEM((2,) + square, bf16),
            pltpu.VMEM((4, NLON, NLAT), f32),
            pltpu.VMEM(half, f32),
            dma((9,)),
            dma((6,)),
        ],
        compiler_params=pltpu.CompilerParams(vmem_limit_bytes=VMEM_LIMIT),
        name="settle",
    )(
        returned.reshape(PLACES, ROWS, COLS),
        deviation.reshape(VARS * LEV, ROWS, COLS),
        back,
        field,
    )
    return result.reshape(VARS, LEV, ROWS, COLS), fields.reshape(1, 4, NLON, NLAT)


def solution(mesh):
    return jax.shard_map(
        local,
        mesh=mesh,
        in_specs=(P(None, None, "sx", "sy"), P(None, None, "sx", "sy"), P(), P(), P()),
        out_specs=(P(None, None, "sx", "sy"), P(("sx", "sy"), None, None, None)),
        check_vma=False,
    )
```

```python
import jax
import jax.numpy as jnp
from jax import lax
from jax.experimental import pallas as pl
from jax.experimental.pallas import tpu as pltpu
from jax.sharding import PartitionSpec as P

MESH = pl.DeviceIdType.MESH
BAND = 12
VARS, LEV, ROWS, COLS = 2, 127, 16, 128
SX, SY = 16, 8
DEVICES = SX * SY
VMEM_LIMIT = 57 * 2**20
NLON, NLAT = 256, 1024
PLACES = 2 * DEVICES
LIFT = VARS * LEV * ROWS


def split(x):
    high = x.astype(jnp.bfloat16)
    return high, (x - high.astype(jnp.float32)).astype(jnp.bfloat16)


def dot(a, b):
    return jnp.dot(a, b, preferred_element_type=jnp.float32)


def dot3(a, b):
    return dot(a[0], b[0]) + (dot(a[0], b[1]) + dot(a[1], b[0]))


def where_to(owner_col, owner_row):
    shape = (PLACES, PLACES)
    down = lax.broadcasted_iota(jnp.int32, shape, 0).astype(jnp.float32)
    over = lax.broadcasted_iota(jnp.int32, shape, 1).astype(jnp.float32)
    one = lambda c: jnp.where(c, 1.0, 0.0)
    same = one(owner_col == owner_row)
    below, above = one(over < down), one(down < over)
    slot_row = jnp.sum(same * above, axis=0, keepdims=True)
    slot_col = jnp.sum(same * below, axis=1, keepdims=True)
    real_row, real_col = one(owner_row >= 0.0), one(owner_col >= 0.0)
    extra_row = real_row * one(slot_row >= 2.0)
    extra_col = real_col * one(slot_col >= 2.0)
    native_row = jnp.where(real_row * (1.0 - extra_row) > 0.0, 2.0 * owner_row + slot_row, -1.0)
    native_col = jnp.where(real_col * (1.0 - extra_col) > 0.0, 2.0 * owner_col + slot_col, -1.0)
    native = one(down == native_row)
    taken_col = jnp.sum(native, axis=1, keepdims=True)
    taken_row = jnp.sum(one(native_col == over), axis=0, keepdims=True)
    rank_row = jnp.sum(extra_col * above, axis=0, keepdims=True)
    free_rank_col = jnp.sum((1.0 - taken_row) * below, axis=1, keepdims=True)
    lent = one(free_rank_col == rank_row) * extra_row * (1.0 - taken_col)
    extra = one(down == 2.0 * owner_row + slot_row - 2.0) * extra_row
    return native + lent, extra, taken_col


def smooth_matrices(long, lon, lat):
    lane = lax.broadcasted_iota(jnp.int32, (8, COLS), 1)
    offset = (lane - BAND).astype(jnp.float32)
    bell = jnp.where(lane <= 2 * BAND, jnp.exp(-(offset * offset) / (2.0 * long * long)), 0.0)
    norm = jnp.sqrt(jnp.sum(bell * bell, axis=1, keepdims=True))[0:1, :]

    def weigh(d):
        near = (d >= -BAND) & (d <= BAND)
        d = d.astype(jnp.float32)
        return jnp.where(near, jnp.exp(-(d * d) / (2.0 * long * long)) / norm, 0.0)

    shape = (NLON, NLON)
    d = lax.broadcasted_iota(jnp.int32, shape, 1) - lax.broadcasted_iota(jnp.int32, shape, 0)
    d = jnp.where(d >= NLON // 2, d - NLON, jnp.where(d < -(NLON // 2), d + NLON, d))
    lon[0], lon[1] = split(weigh(d))
    shape = (512, 256)
    d = lax.broadcasted_iota(jnp.int32, shape, 0) - 128 - lax.broadcasted_iota(jnp.int32, shape, 1)
    lat[0], lat[1] = split(weigh(d))


def travel_kernel(
    control_hbm, deviation_hbm, vertical_hbm, length_hbm, owners_hbm,
    returned, field_hbm, back_hbm,
    control, deviation, vertical_ref, length_ref, owners_ref, scaled, pieces, matrix, length_row_ref,
    home, extra, outgoing, along, lon, lat, field, back,
    in_sem, send_sem, home_sem, extra_sem, back_sem, own_sem, out_sem, column_sem,
):
    mx, my = lax.axis_index("sx"), lax.axis_index("sy")
    me = mx * SY + my
    here = my * SX + mx
    z, y, x, core = mx // 4, mx % 4, my // 2, my % 2

    def partner(step):
        k = DEVICES - step
        px = ((z + (k // 4) % 4) % 4) * 4 + (y + (k // 16) % 4) % 4
        py = ((x + k % 4) % 4) * 2 + (core + k // 64) % 2
        return px, py

    cut = LIFT // 2
    small = []
    for at, (src, dst) in enumerate(
        ((owners_hbm, owners_ref), (vertical_hbm, vertical_ref), (length_hbm, length_ref))
    ):
        small.append(pltpu.make_async_copy(src, dst, in_sem.at[4 + at]))
        small[-1].start()
    loads = []
    for part in range(2):
        rows = pl.ds(part * cut, cut)
        for at, (src, dst) in enumerate(((control_hbm, control), (deviation_hbm, deviation))):
            loads.append(pltpu.make_async_copy(src.at[rows], dst.at[rows], in_sem.at[2 * part + at]))
    for load in loads:
        load.start()

    barrier = pltpu.get_barrier_semaphore()

    @pl.loop(1, SX)
    def _(step):
        pl.semaphore_signal(barrier, inc=1, device_id=(lax.rem(mx + step, SX), my), device_id_type=MESH)

    @pl.loop(1, SY)
    def _(step):
        pl.semaphore_signal(barrier, inc=1, device_id=(mx, lax.rem(my + step, SY)), device_id_type=MESH)

    control[LIFT:, :] = jnp.zeros((ROWS, COLS), jnp.float32)
    deviation[LIFT:, :] = jnp.zeros((ROWS, COLS), jnp.float32)
    length_row_ref[...] = jnp.ones((1, PLACES), jnp.float32)
    matrix[...] = jnp.zeros((PLACES, PLACES), jnp.float32)
    for load in small:
        load.wait()
    for v in range(VARS):
        length_row_ref[:, v * 128 : v * 128 + LEV] = length_ref[v : v + 1, :]
        matrix[v * 128 : v * 128 + LEV, v * 128 : v * 128 + LEV] = vertical_ref[:, v, :]
    slab = lax.broadcasted_iota(jnp.int32, (PLACES, VARS * LEV), 0)
    level = slab % 128
    number = jnp.where(level < LEV, slab - slab // 128, -1)
    listed = lax.broadcasted_iota(jnp.int32, (PLACES, VARS * LEV), 1) == number
    owners = owners_ref[...].astype(jnp.float32)
    owner_col = jnp.sum(jnp.where(listed, owners + 1.0, 0.0), axis=1, keepdims=True) - 1.0
    shape = (PLACES, PLACES)
    down = lax.broadcasted_iota(jnp.int32, shape, 0)
    over = lax.broadcasted_iota(jnp.int32, shape, 1)
    owner_row = jnp.sum(jnp.where(down == over, owner_col, 0.0), axis=0, keepdims=True)
    home_hot, extra_hot, taken_col = where_to(owner_col, owner_row)
    high, low = split(matrix[...])

    def lift(hot, first):
        hot = hot.astype(jnp.bfloat16)
        rows = (dot(hot, high).astype(jnp.bfloat16), dot(hot, low).astype(jnp.bfloat16))
        for i in range(0, ROWS, 2):
            lifted = dot3(rows, (scaled[0, i // 2], scaled[1, i // 2]))
            for r in (0, 1):
                at = pl.ds(first * ROWS + i + r, PLACES, stride=ROWS)
                pieces[at, :] = lifted[:, r * COLS : (r + 1) * COLS]

    def two(first, device):
        return pieces.at[pl.ds((first + 2 * device) * ROWS, 2 * ROWS)]

    def scatter(first, into, sem):
        @pl.loop(1, DEVICES)
        def _(step):
            px, py = partner(step)
            pltpu.make_async_remote_copy(
                src_ref=two(first, px * SY + py),
                dst_ref=into.at[here],
                send_sem=send_sem,
                recv_sem=sem,
                device_id=(px, py),
                device_id_type=MESH,
            ).start()

    pl.semaphore_wait(barrier, SX + SY - 2)

    @pl.loop(1, SY)
    def _(step):
        pl.semaphore_signal(column_sem, inc=1, device_id=(mx, lax.rem(my + step, SY)), device_id_type=MESH)

    for load in loads:
        load.wait()
    for i in range(0, ROWS, 2):
        sides = []
        for r in (i, i + 1):
            halves = []
            for v in range(VARS):
                at = pl.ds(v * LEV * ROWS + r, 128, stride=ROWS)
                halves.append(control[at, :] * deviation[at, :])
            sides.append(jnp.concatenate(halves, axis=0))
        scaled[0, i // 2], scaled[1, i // 2] = split(jnp.concatenate(sides, axis=1))

    lift(home_hot, 0)
    pl.semaphore_wait(column_sem, SY - 1)
    scatter(0, home, home_sem)
    own_home = pltpu.make_async_copy(two(0, me), home.at[here], own_sem.at[0])
    own_home.start()
    lift(extra_hot, PLACES)
    scatter(PLACES, extra, extra_sem)
    own_extra = pltpu.make_async_copy(two(PLACES, me), extra.at[here], own_sem.at[1])
    own_extra.start()

    turned_high, turned_low = split(matrix[...].T)
    home_turned = home_hot.T.astype(jnp.bfloat16)
    back[0] = dot(turned_high, home_turned).astype(jnp.bfloat16)
    back[1] = dot(turned_low, home_turned).astype(jnp.bfloat16)
    out = [pltpu.make_async_copy(back, back_hbm, out_sem.at[4])]
    out[0].start()
    length_row = length_row_ref[...]
    place = lax.broadcasted_iota(jnp.int32, (PLACES, 1), 0).astype(jnp.float32)
    owned = []
    for at, hot in ((0, home_hot), (2, extra_hot)):
        used = jnp.sum(hot, axis=1, keepdims=True)
        long = jnp.sum(hot * length_row, axis=1, keepdims=True) + (1.0 - used)
        for h in range(2):
            mine = jnp.where(place == (2 * me + h).astype(jnp.float32), 1.0, 0.0)
            smooth_matrices(jnp.sum(mine * long, axis=0, keepdims=True), lon.at[at + h], lat.at[at + h])
            if at == 0:
                owned.append(jnp.sum(mine * taken_col, axis=0, keepdims=True))

    def smooth(h, source, keep):
        for t in range(4):
            blocks = [
                source[pl.ds((2 * t + b) * SX, SX), h * ROWS : (h + 1) * ROWS].reshape(NLON, COLS) for b in range(2)
            ]
            lifted = split(jnp.concatenate(blocks, axis=1))
            along[:, t * 256 : (t + 1) * 256] = dot3((lon[keep, 0], lon[keep, 1]), lifted)
        for t in range(4):
            begin, end = max(0, 256 * t - 128), min(NLAT, 256 * t + 384)
            taps = pl.ds(begin - (256 * t - 128), end - begin)
            done = dot3(split(along[:, begin:end]), (lat[keep, 0, taps, :], lat[keep, 1, taps, :]))
            if keep < 2:
                field[keep, :, t * 256 : (t + 1) * 256] = done * owned[keep]
                for b in range(2):
                    outgoing[pl.ds((2 * t + b) * SX, SX), h * ROWS : (h + 1) * ROWS] = done[
                        :, b * COLS : (b + 1) * COLS
                    ].reshape(SX, ROWS, COLS)
            else:
                field[keep, :, t * 256 : (t + 1) * 256] = done

    own_home.wait()
    pltpu.make_async_copy(home.at[pl.ds(0, DEVICES - 1)], home.at[pl.ds(0, DEVICES - 1)], home_sem).wait()
    for h in range(2):
        smooth(h, home, h)
    into = returned.at[pl.ds(2 * ROWS * me, 2 * ROWS)]
    own_back = pltpu.make_async_copy(outgoing.at[here], into, own_sem.at[2])
    own_back.start()

    @pl.loop(1, DEVICES)
    def _(step):
        px, py = partner(step)
        pltpu.make_async_remote_copy(
            src_ref=outgoing.at[py * SX + px],
            dst_ref=into,
            send_sem=send_sem,
            recv_sem=back_sem,
            device_id=(px, py),
            device_id_type=MESH,
        ).start()

    def write(h):
        out.append(pltpu.make_async_copy(field.at[h], field_hbm.at[h], out_sem.at[h]))
        out[-1].start()

    for h in range(2):
        write(h)
    own_extra.wait()
    pltpu.make_async_copy(extra.at[pl.ds(0, DEVICES - 1)], extra.at[pl.ds(0, DEVICES - 1)], extra_sem).wait()
    for h in range(2):
        smooth(h, extra, 2 + h)
        write(2 + h)
    own_back.wait()
    for copy in out:
        copy.wait()
    arrived = returned.at[pl.ds(0, 2 * ROWS * (DEVICES - 1))]
    pltpu.make_async_copy(arrived, arrived, back_sem).wait()
    for _ in range(3):
        pltpu.make_async_copy(arrived, arrived, send_sem).wait()


def settle_kernel(
    returned_hbm, deviation_hbm, back_hbm, field_hbm,
    result_hbm, fields_hbm,
    returned, deviation, back, field, result, in_sem, out_sem,
):
    half = ROWS // 2
    loads = [pltpu.make_async_copy(back_hbm, back, in_sem.at[0])]
    for part in range(2):
        rows = pl.ds(part * half, half)
        at = 1 + 2 * part
        loads.append(pltpu.make_async_copy(returned_hbm.at[:, rows], returned.at[part], in_sem.at[at]))
        loads.append(pltpu.make_async_copy(deviation_hbm.at[:, rows], deviation.at[part], in_sem.at[at + 1]))
    slots = [pltpu.make_async_copy(field_hbm.at[h], field.at[h], in_sem.at[5 + h]) for h in range(4)]
    for load in loads + slots:
        load.start()
    out = []

    def write(src, dst):
        out.append(pltpu.make_async_copy(src, dst, out_sem.at[len(out)]))
        out[-1].start()

    loads[0].wait()
    ways = (back[0], back[1])
    for part in range(2):
        for load in loads[1 + 2 * part : 3 + 2 * part]:
            load.wait()
        arrived = returned.at[part].reshape(PLACES * half, COLS)
        spread = deviation.at[part].reshape(VARS * LEV * half, COLS)
        settled_to = result.at[part].reshape(VARS * LEV * half, COLS)
        for i in range(0, half, 2):
            sides = [arrived[pl.ds(i + r, PLACES, stride=half), :] for r in range(2)]
            settled = dot3(ways, split(jnp.concatenate(sides, axis=1)))
            for r in range(2):
                for v in range(VARS):
                    at = pl.ds(v * LEV * half + i + r, LEV, stride=half)
                    settled_to[at, :] = spread[at, :] * settled[v * 128 : v * 128 + LEV, r * COLS : (r + 1) * COLS]
            slot = part * 2 + i // 4
            if i % 4 == 0:
                slots[slot].wait()
                write(field.at[slot], fields_hbm.at[slot])
        write(result.at[part], result_hbm.at[:, pl.ds(part * half, half)])
    for copy in out:
        copy.wait()


def local(control, deviation, vertical, length, owners):
    f32, bf16 = jnp.float32, jnp.bfloat16
    hbm = pl.BlockSpec(memory_space=pl.ANY)
    dma = pltpu.SemaphoreType.DMA
    flat, square = (LIFT, COLS), (PLACES, PLACES)
    block = (DEVICES, 2 * ROWS, COLS)
    deviation = deviation.reshape(flat)
    returned, field, back = pl.pallas_call(
        travel_kernel,
        out_shape=[
            jax.ShapeDtypeStruct((PLACES * ROWS, COLS), f32),
            jax.ShapeDtypeStruct((4, NLON, NLAT), f32),
            jax.ShapeDtypeStruct((2,) + square, bf16),
        ],
        in_specs=[hbm] * 5,
        out_specs=[hbm] * 3,
        scratch_shapes=[
            pltpu.VMEM((LIFT + ROWS, COLS), f32),
            pltpu.VMEM((LIFT + ROWS, COLS), f32),
            pltpu.VMEM((LEV, VARS, LEV), f32),
            pltpu.VMEM((VARS, LEV), f32),
            pltpu.VMEM((1, VARS * LEV), jnp.int32),
            pltpu.VMEM((2, ROWS // 2, PLACES, 2 * COLS), bf16),
            pltpu.VMEM((2 * PLACES * ROWS, COLS), f32),
            pltpu.VMEM(square, f32),
            pltpu.VMEM((1, PLACES), f32),
            pltpu.VMEM(block, f32),
            pltpu.VMEM(block, f32),
            pltpu.VMEM(block, f32),
            pltpu.VMEM((NLON, NLAT), f32),
            pltpu.VMEM((4, 2, NLON, NLON), bf16),
            pltpu.VMEM((4, 2, 512, 256), bf16),
            pltpu.VMEM((4, NLON, NLAT), f32),
            pltpu.VMEM((2,) + square, bf16),
            dma((7,)), dma, dma, dma, dma, dma((3,)), dma((5,)),
            pltpu.SemaphoreType.REGULAR,
        ],
        compiler_params=pltpu.CompilerParams(
            collective_id=0, has_side_effects=True, vmem_limit_bytes=VMEM_LIMIT
        ),
        name="travel",
    )(control.reshape(flat), deviation, vertical.transpose(1, 0, 2), length, owners.reshape(1, VARS * LEV))

    half = (2, VARS * LEV, ROWS // 2, COLS)
    result, fields = pl.pallas_call(
        settle_kernel,
        out_shape=[
            jax.ShapeDtypeStruct((VARS * LEV, ROWS, COLS), f32),
            jax.ShapeDtypeStruct((4, NLON, NLAT), f32),
        ],
        in_specs=[hbm] * 4,
        out_specs=[hbm] * 2,
        scratch_shapes=[
            pltpu.VMEM((2, PLACES, ROWS // 2, COLS), f32),
            pltpu.VMEM(half, f32),
            pltpu.VMEM((2,) + square, bf16),
            pltpu.VMEM((4, NLON, NLAT), f32),
            pltpu.VMEM(half, f32),
            dma((9,)),
            dma((6,)),
        ],
        compiler_params=pltpu.CompilerParams(vmem_limit_bytes=VMEM_LIMIT),
        name="settle",
    )(
        returned.reshape(PLACES, ROWS, COLS),
        deviation.reshape(VARS * LEV, ROWS, COLS),
        back,
        field,
    )
    return result.reshape(VARS, LEV, ROWS, COLS), fields.reshape(1, 4, NLON, NLAT)


def solution(mesh):
    return jax.shard_map(
        local,
        mesh=mesh,
        in_specs=(P(None, None, "sx", "sy"), P(None, None, "sx", "sy"), P(), P(), P()),
        out_specs=(P(None, None, "sx", "sy"), P(("sx", "sy"), None, None, None)),
        check_vma=False,
    )
```

```python
import jax
import jax.numpy as jnp
from jax import lax
from jax.experimental import pallas as pl
from jax.experimental.pallas import tpu as pltpu
from jax.sharding import PartitionSpec as P

MESH = pl.DeviceIdType.MESH
BAND = 12
VARS, LEV, ROWS, COLS = 2, 127, 16, 128
SX, SY = 16, 8
DEVICES = SX * SY
VMEM_LIMIT = 57 * 2**20
SETTLE_LIMIT = 103 * 2**19
NLON, NLAT = 256, 1024
PLACES = 2 * DEVICES
LIFT = VARS * LEV * ROWS


def split(x):
    high = x.astype(jnp.bfloat16)
    return high, (x - high.astype(jnp.float32)).astype(jnp.bfloat16)


def dot(a, b):
    return jnp.dot(a, b, preferred_element_type=jnp.float32)


def dot3(a, b):
    return dot(a[0], b[0]) + (dot(a[0], b[1]) + dot(a[1], b[0]))


def where_to(owner_col, owner_row):
    shape = (PLACES, PLACES)
    down = lax.broadcasted_iota(jnp.int32, shape, 0).astype(jnp.float32)
    over = lax.broadcasted_iota(jnp.int32, shape, 1).astype(jnp.float32)
    one = lambda c: jnp.where(c, 1.0, 0.0)
    same = one(owner_col == owner_row)
    below, above = one(over < down), one(down < over)
    slot_row = jnp.sum(same * above, axis=0, keepdims=True)
    slot_col = jnp.sum(same * below, axis=1, keepdims=True)
    real_row, real_col = one(owner_row >= 0.0), one(owner_col >= 0.0)
    extra_row = real_row * one(slot_row >= 2.0)
    extra_col = real_col * one(slot_col >= 2.0)
    native_row = jnp.where(real_row * (1.0 - extra_row) > 0.0, 2.0 * owner_row + slot_row, -1.0)
    native_col = jnp.where(real_col * (1.0 - extra_col) > 0.0, 2.0 * owner_col + slot_col, -1.0)
    native = one(down == native_row)
    taken_col = jnp.sum(native, axis=1, keepdims=True)
    taken_row = jnp.sum(one(native_col == over), axis=0, keepdims=True)
    rank_row = jnp.sum(extra_col * above, axis=0, keepdims=True)
    free_rank_col = jnp.sum((1.0 - taken_row) * below, axis=1, keepdims=True)
    lent = one(free_rank_col == rank_row) * extra_row * (1.0 - taken_col)
    extra = one(down == 2.0 * owner_row + slot_row - 2.0) * extra_row
    return native + lent, extra, taken_col


def smooth_matrices(long, lon, lat):
    lane = lax.broadcasted_iota(jnp.int32, (8, COLS), 1)
    offset = (lane - BAND).astype(jnp.float32)
    bell = jnp.where(lane <= 2 * BAND, jnp.exp(-(offset * offset) / (2.0 * long * long)), 0.0)
    norm = jnp.sqrt(jnp.sum(bell * bell, axis=1, keepdims=True))[0:1, :]

    def weigh(d):
        near = (d >= -BAND) & (d <= BAND)
        d = d.astype(jnp.float32)
        return jnp.where(near, jnp.exp(-(d * d) / (2.0 * long * long)) / norm, 0.0)

    shape = (NLON, NLON)
    d = lax.broadcasted_iota(jnp.int32, shape, 1) - lax.broadcasted_iota(jnp.int32, shape, 0)
    d = jnp.where(d >= NLON // 2, d - NLON, jnp.where(d < -(NLON // 2), d + NLON, d))
    lon[0], lon[1] = split(weigh(d))
    shape = (512, 256)
    d = lax.broadcasted_iota(jnp.int32, shape, 0) - 128 - lax.broadcasted_iota(jnp.int32, shape, 1)
    lat[0], lat[1] = split(weigh(d))


def travel_kernel(
    control_hbm, deviation_hbm, vertical_hbm, length_hbm, owners_hbm,
    returned, field_hbm,
    control, deviation, vertical_ref, length_ref, owners_ref, scaled, pieces, matrix, length_row_ref,
    home, extra, outgoing, along, lon, lat, field, back,
    in_sem, send_sem, home_sem, extra_sem, back_sem, own_sem, out_sem, column_sem,
):
    mx, my = lax.axis_index("sx"), lax.axis_index("sy")
    me = mx * SY + my
    here = my * SX + mx
    z, y, x, core = mx // 4, mx % 4, my // 2, my % 2

    def partner(step):
        k = DEVICES - step
        px = ((z + (k // 4) % 4) % 4) * 4 + (y + (k // 16) % 4) % 4
        py = ((x + k % 4) % 4) * 2 + (core + k // 64) % 2
        return px, py

    cut = LIFT // 2
    small = []
    for at, (src, dst) in enumerate(
        ((owners_hbm, owners_ref), (vertical_hbm, vertical_ref), (length_hbm, length_ref))
    ):
        small.append(pltpu.make_async_copy(src, dst, in_sem.at[4 + at]))
        small[-1].start()
    loads = []
    for part in range(2):
        rows = pl.ds(part * cut, cut)
        for at, (src, dst) in enumerate(((control_hbm, control), (deviation_hbm, deviation))):
            loads.append(pltpu.make_async_copy(src.at[rows], dst.at[rows], in_sem.at[2 * part + at]))
    for load in loads:
        load.start()

    barrier = pltpu.get_barrier_semaphore()

    @pl.loop(1, SX)
    def _(step):
        pl.semaphore_signal(barrier, inc=1, device_id=(lax.rem(mx + step, SX), my), device_id_type=MESH)

    @pl.loop(1, SY)
    def _(step):
        pl.semaphore_signal(barrier, inc=1, device_id=(mx, lax.rem(my + step, SY)), device_id_type=MESH)

    control[LIFT:, :] = jnp.zeros((ROWS, COLS), jnp.float32)
    deviation[LIFT:, :] = jnp.zeros((ROWS, COLS), jnp.float32)
    length_row_ref[...] = jnp.ones((1, PLACES), jnp.float32)
    matrix[...] = jnp.zeros((PLACES, PLACES), jnp.float32)
    for load in small:
        load.wait()
    for v in range(VARS):
        length_row_ref[:, v * 128 : v * 128 + LEV] = length_ref[v : v + 1, :]
        matrix[v * 128 : v * 128 + LEV, v * 128 : v * 128 + LEV] = vertical_ref[:, v, :]
    slab = lax.broadcasted_iota(jnp.int32, (PLACES, VARS * LEV), 0)
    level = slab % 128
    number = jnp.where(level < LEV, slab - slab // 128, -1)
    listed = lax.broadcasted_iota(jnp.int32, (PLACES, VARS * LEV), 1) == number
    owners = owners_ref[...].astype(jnp.float32)
    owner_col = jnp.sum(jnp.where(listed, owners + 1.0, 0.0), axis=1, keepdims=True) - 1.0
    shape = (PLACES, PLACES)
    down = lax.broadcasted_iota(jnp.int32, shape, 0)
    over = lax.broadcasted_iota(jnp.int32, shape, 1)
    owner_row = jnp.sum(jnp.where(down == over, owner_col, 0.0), axis=0, keepdims=True)
    home_hot, extra_hot, taken_col = where_to(owner_col, owner_row)
    high, low = split(matrix[...])

    def lift(hot, first):
        hot = hot.astype(jnp.bfloat16)
        rows = (dot(hot, high).astype(jnp.bfloat16), dot(hot, low).astype(jnp.bfloat16))
        for i in range(0, ROWS, 2):
            lifted = dot3(rows, (scaled[0, i // 2], scaled[1, i // 2]))
            for r in (0, 1):
                at = pl.ds(first * ROWS + i + r, hot.shape[0], stride=ROWS)
                pieces[at, :] = lifted[:, r * COLS : (r + 1) * COLS]

    def two(first, device):
        return pieces.at[pl.ds((first + 2 * device) * ROWS, 2 * ROWS)]

    def scatter(first, into, sem):
        @pl.loop(1, DEVICES)
        def _(step):
            px, py = partner(step)
            pltpu.make_async_remote_copy(
                src_ref=two(first, px * SY + py),
                dst_ref=into.at[here],
                send_sem=send_sem,
                recv_sem=sem,
                device_id=(px, py),
                device_id_type=MESH,
            ).start()

    pl.semaphore_wait(barrier, SX + SY - 2)

    @pl.loop(1, SY)
    def _(step):
        pl.semaphore_signal(column_sem, inc=1, device_id=(mx, lax.rem(my + step, SY)), device_id_type=MESH)

    for load in loads:
        load.wait()
    for i in range(0, ROWS, 2):
        sides = []
        for r in (i, i + 1):
            halves = []
            for v in range(VARS):
                at = pl.ds(v * LEV * ROWS + r, 128, stride=ROWS)
                halves.append(control[at, :] * deviation[at, :])
            sides.append(jnp.concatenate(halves, axis=0))
        scaled[0, i // 2], scaled[1, i // 2] = split(jnp.concatenate(sides, axis=1))

    lift(home_hot, 0)
    pl.semaphore_wait(column_sem, SY - 1)
    scatter(0, home, home_sem)
    own_home = pltpu.make_async_copy(two(0, me), home.at[here], own_sem.at[0])
    own_home.start()
    lift(extra_hot, PLACES)
    scatter(PLACES, extra, extra_sem)
    own_extra = pltpu.make_async_copy(two(PLACES, me), extra.at[here], own_sem.at[1])
    own_extra.start()

    turned_high, turned_low = split(matrix[...].T)
    home_turned = home_hot.T.astype(jnp.bfloat16)
    whole = dot(turned_high, home_turned) + dot(turned_low, home_turned)
    for side in range(2):
        back[side * PLACES : (side + 1) * PLACES, :] = whole[:, side * COLS : (side + 1) * COLS]
    out = [pltpu.make_async_copy(back, returned.at[pl.ds(PLACES * ROWS, 2 * PLACES)], out_sem.at[4])]
    out[0].start()
    length_row = length_row_ref[...]
    place = lax.broadcasted_iota(jnp.int32, (PLACES, 1), 0).astype(jnp.float32)
    owned = []
    for at, hot in ((0, home_hot), (2, extra_hot)):
        used = jnp.sum(hot, axis=1, keepdims=True)
        long = jnp.sum(hot * length_row, axis=1, keepdims=True) + (1.0 - used)
        for h in range(2):
            mine = jnp.where(place == (2 * me + h).astype(jnp.float32), 1.0, 0.0)
            smooth_matrices(jnp.sum(mine * long, axis=0, keepdims=True), lon.at[at + h], lat.at[at + h])
            if at == 0:
                owned.append(jnp.sum(mine * taken_col, axis=0, keepdims=True))

    def smooth(h, source, keep):
        for t in range(4):
            blocks = [
                source[pl.ds((2 * t + b) * SX, SX), h * ROWS : (h + 1) * ROWS].reshape(NLON, COLS) for b in range(2)
            ]
            lifted = split(jnp.concatenate(blocks, axis=1))
            along[:, t * 256 : (t + 1) * 256] = dot3((lon[keep, 0], lon[keep, 1]), lifted)
        for t in range(4):
            begin, end = max(0, 256 * t - 128), min(NLAT, 256 * t + 384)
            taps = pl.ds(begin - (256 * t - 128), end - begin)
            done = dot3(split(along[:, begin:end]), (lat[keep, 0, taps, :], lat[keep, 1, taps, :]))
            if keep < 2:
                field[keep, :, t * 256 : (t + 1) * 256] = done * owned[keep]
                for b in range(2):
                    outgoing[pl.ds((2 * t + b) * SX, SX), h * ROWS : (h + 1) * ROWS] = done[
                        :, b * COLS : (b + 1) * COLS
                    ].reshape(SX, ROWS, COLS)
            else:
                field[keep, :, t * 256 : (t + 1) * 256] = done

    own_home.wait()
    pltpu.make_async_copy(home.at[pl.ds(0, DEVICES - 1)], home.at[pl.ds(0, DEVICES - 1)], home_sem).wait()
    for h in range(2):
        smooth(h, home, h)
    into = returned.at[pl.ds(2 * ROWS * me, 2 * ROWS)]
    own_back = pltpu.make_async_copy(outgoing.at[here], into, own_sem.at[2])
    own_back.start()

    @pl.loop(1, DEVICES)
    def _(step):
        px, py = partner(step)
        pltpu.make_async_remote_copy(
            src_ref=outgoing.at[py * SX + px],
            dst_ref=into,
            send_sem=send_sem,
            recv_sem=back_sem,
            device_id=(px, py),
            device_id_type=MESH,
        ).start()

    def write(h):
        out.append(pltpu.make_async_copy(field.at[h], field_hbm.at[h], out_sem.at[h]))
        out[-1].start()

    for h in range(2):
        write(h)
    own_extra.wait()
    pltpu.make_async_copy(extra.at[pl.ds(0, DEVICES - 1)], extra.at[pl.ds(0, DEVICES - 1)], extra_sem).wait()
    for h in range(2):
        smooth(h, extra, 2 + h)
        write(2 + h)
    own_back.wait()
    for copy in out:
        copy.wait()
    arrived = returned.at[pl.ds(0, 2 * ROWS * (DEVICES - 1))]
    pltpu.make_async_copy(arrived, arrived, back_sem).wait()
    for _ in range(3):
        pltpu.make_async_copy(arrived, arrived, send_sem).wait()


def settle_kernel(
    returned_hbm, deviation_hbm, field_hbm,
    result_hbm, fields_hbm,
    returned, deviation, back, field, result, in_sem, out_sem,
):
    half = ROWS // 2
    tail = pl.ds(PLACES, 2 * PLACES // ROWS)
    loads = [pltpu.make_async_copy(returned_hbm.at[tail], back, in_sem.at[0])]
    for part in range(2):
        rows = pl.ds(part * half, half)
        at = 1 + 2 * part
        loads.append(pltpu.make_async_copy(returned_hbm.at[pl.ds(0, PLACES), rows], returned.at[part], in_sem.at[at]))
        loads.append(pltpu.make_async_copy(deviation_hbm.at[:, rows], deviation.at[part], in_sem.at[at + 1]))
    slots = [pltpu.make_async_copy(field_hbm.at[h], field.at[h], in_sem.at[5 + h]) for h in range(4)]
    for load in loads + slots:
        load.start()
    out = []

    def write(src, dst):
        out.append(pltpu.make_async_copy(src, dst, out_sem.at[len(out)]))
        out[-1].start()

    loads[0].wait()
    flat = back[...].reshape(2 * PLACES, COLS)
    ways = split(jnp.concatenate([flat[:PLACES], flat[PLACES:]], axis=1))
    for part in range(2):
        for load in loads[1 + 2 * part : 3 + 2 * part]:
            load.wait()
        arrived = returned.at[part].reshape(PLACES * half, COLS)
        spread = deviation.at[part].reshape(VARS * LEV * half, COLS)
        settled_to = result.at[part].reshape(VARS * LEV * half, COLS)
        for i in range(0, half, 2):
            sides = [arrived[pl.ds(i + r, PLACES, stride=half), :] for r in range(2)]
            settled = dot3(ways, split(jnp.concatenate(sides, axis=1)))
            for r in range(2):
                for v in range(VARS):
                    at = pl.ds(v * LEV * half + i + r, LEV, stride=half)
                    settled_to[at, :] = spread[at, :] * settled[v * 128 : v * 128 + LEV, r * COLS : (r + 1) * COLS]
            slot = part * 2 + i // 4
            if i % 4 == 0:
                slots[slot].wait()
                write(field.at[slot], fields_hbm.at[slot])
        write(result.at[part], result_hbm.at[:, pl.ds(part * half, half)])
    for copy in out:
        copy.wait()


def local(control, deviation, vertical, length, owners):
    f32, bf16 = jnp.float32, jnp.bfloat16
    hbm = pl.BlockSpec(memory_space=pl.ANY)
    dma = pltpu.SemaphoreType.DMA
    flat, square = (LIFT, COLS), (PLACES, PLACES)
    block = (DEVICES, 2 * ROWS, COLS)
    deviation = deviation.reshape(flat)
    returned, field = pl.pallas_call(
        travel_kernel,
        out_shape=[
            jax.ShapeDtypeStruct((PLACES * ROWS + 2 * PLACES, COLS), f32),
            jax.ShapeDtypeStruct((4, NLON, NLAT), f32),
        ],
        in_specs=[hbm] * 5,
        out_specs=[hbm] * 2,
        scratch_shapes=[
            pltpu.VMEM((LIFT + ROWS, COLS), f32),
            pltpu.VMEM((LIFT + ROWS, COLS), f32),
            pltpu.VMEM((LEV, VARS, LEV), f32),
            pltpu.VMEM((VARS, LEV), f32),
            pltpu.VMEM((1, VARS * LEV), jnp.int32),
            pltpu.VMEM((2, ROWS // 2, PLACES, 2 * COLS), bf16),
            pltpu.VMEM((2 * PLACES * ROWS, COLS), f32),
            pltpu.VMEM(square, f32),
            pltpu.VMEM((1, PLACES), f32),
            pltpu.VMEM(block, f32),
            pltpu.VMEM(block, f32),
            pltpu.VMEM(block, f32),
            pltpu.VMEM((NLON, NLAT), f32),
            pltpu.VMEM((4, 2, NLON, NLON), bf16),
            pltpu.VMEM((4, 2, 512, 256), bf16),
            pltpu.VMEM((4, NLON, NLAT), f32),
            pltpu.VMEM((2 * PLACES, COLS), f32),
            dma((7,)), dma, dma, dma, dma, dma((3,)), dma((5,)),
            pltpu.SemaphoreType.REGULAR,
        ],
        compiler_params=pltpu.CompilerParams(
            collective_id=0, has_side_effects=True, vmem_limit_bytes=VMEM_LIMIT
        ),
        name="travel",
    )(control.reshape(flat), deviation, vertical.transpose(1, 0, 2), length, owners.reshape(1, VARS * LEV))

    half = (2, VARS * LEV, ROWS // 2, COLS)
    result, fields = pl.pallas_call(
        settle_kernel,
        out_shape=[
            jax.ShapeDtypeStruct((VARS * LEV, ROWS, COLS), f32),
            jax.ShapeDtypeStruct((4, NLON, NLAT), f32),
        ],
        in_specs=[hbm] * 3,
        out_specs=[hbm] * 2,
        scratch_shapes=[
            pltpu.VMEM((2, PLACES, ROWS // 2, COLS), f32),
            pltpu.VMEM(half, f32),
            pltpu.VMEM((2 * PLACES // ROWS, ROWS, COLS), f32),
            pltpu.VMEM((4, NLON, NLAT), f32),
            pltpu.VMEM(half, f32),
            dma((9,)),
            dma((6,)),
        ],
        compiler_params=pltpu.CompilerParams(vmem_limit_bytes=SETTLE_LIMIT),
        name="settle",
    )(
        returned.reshape(PLACES + 2 * PLACES // ROWS, ROWS, COLS),
        deviation.reshape(VARS * LEV, ROWS, COLS),
        field,
    )
    return result.reshape(VARS, LEV, ROWS, COLS), fields.reshape(1, 4, NLON, NLAT)


def solution(mesh):
    return jax.shard_map(
        local,
        mesh=mesh,
        in_specs=(P(None, None, "sx", "sy"), P(None, None, "sx", "sy"), P(), P(), P()),
        out_specs=(P(None, None, "sx", "sy"), P(("sx", "sy"), None, None, None)),
        check_vma=False,
    )
```

```python
import jax
import jax.numpy as jnp
from jax import lax
from jax.experimental import pallas as pl
from jax.experimental.pallas import tpu as pltpu
from jax.sharding import PartitionSpec as P

MESH = pl.DeviceIdType.MESH
BAND = 12
VARS, LEV, ROWS, COLS = 2, 127, 16, 128
SX, SY = 16, 8
DEVICES = SX * SY
VMEM_LIMIT = 57 * 2**20
SETTLE_LIMIT = 103 * 2**19
NLON, NLAT = 256, 1024
PLACES = 2 * DEVICES
LIFT = VARS * LEV * ROWS


def split(x):
    high = x.astype(jnp.bfloat16)
    return high, (x - high.astype(jnp.float32)).astype(jnp.bfloat16)


def dot(a, b):
    return jnp.dot(a, b, preferred_element_type=jnp.float32)


def dot3(a, b):
    return dot(a[0], b[0]) + (dot(a[0], b[1]) + dot(a[1], b[0]))


def where_to(owner_col, owner_row, label):
    shape = (PLACES, PLACES)
    down = lax.broadcasted_iota(jnp.int32, shape, 0).astype(jnp.float32)
    over = lax.broadcasted_iota(jnp.int32, shape, 1).astype(jnp.float32)
    one = lambda c: jnp.where(c, 1.0, 0.0)
    device_col, device_row = jnp.floor(label / 2.0), jnp.floor(over[:1] / 2.0)
    count_col = jnp.sum(one(owner_row == device_col), axis=1, keepdims=True)
    count_row = jnp.sum(one(owner_col == device_row), axis=0, keepdims=True)
    taken_col = one(count_col > label - 2.0 * device_col)
    taken_row = one(count_row > over[:1] - 2.0 * device_row)
    free_rank_col = jnp.sum((1.0 - taken_row) * one(over < label), axis=1, keepdims=True)
    same = one(owner_col == owner_row)
    above = one(down < over)
    slot_row = jnp.sum(same * above, axis=0, keepdims=True)
    slot_col = jnp.sum(same * one(over < down), axis=1, keepdims=True)
    extra_row = one(owner_row >= 0.0) * one(slot_row >= 2.0)
    extra_col = one(owner_col >= 0.0) * one(slot_col >= 2.0)
    place_row = 2.0 * owner_row + slot_row
    rank_row = jnp.sum(extra_col * above, axis=0, keepdims=True)
    native = one(label == jnp.where(owner_row >= 0.0, place_row, -1.0)) * (1.0 - extra_row)
    lent = one(free_rank_col == rank_row) * extra_row * (1.0 - taken_col)
    extra = one(label == place_row - 2.0) * extra_row
    return native + lent, extra, taken_col


def smooth_matrices(long, lon, lat):
    lane = lax.broadcasted_iota(jnp.int32, (8, COLS), 1)
    offset = (lane - BAND).astype(jnp.float32)
    bell = jnp.where(lane <= 2 * BAND, jnp.exp(-(offset * offset) / (2.0 * long * long)), 0.0)
    norm = jnp.sqrt(jnp.sum(bell * bell, axis=1, keepdims=True))[0:1, :]

    def weigh(d):
        near = (d >= -BAND) & (d <= BAND)
        d = d.astype(jnp.float32)
        return jnp.where(near, jnp.exp(-(d * d) / (2.0 * long * long)) / norm, 0.0)

    shape = (NLON, NLON)
    d = lax.broadcasted_iota(jnp.int32, shape, 1) - lax.broadcasted_iota(jnp.int32, shape, 0)
    d = jnp.where(d >= NLON // 2, d - NLON, jnp.where(d < -(NLON // 2), d + NLON, d))
    lon[0], lon[1] = split(weigh(d))
    shape = (512, 256)
    d = lax.broadcasted_iota(jnp.int32, shape, 0) - 128 - lax.broadcasted_iota(jnp.int32, shape, 1)
    lat[0], lat[1] = split(weigh(d))


def travel_kernel(
    control_hbm, deviation_hbm, vertical_hbm, length_hbm, owners_hbm,
    returned, field_hbm,
    control, deviation, vertical_ref, length_ref, owners_ref, scaled, pieces, matrix, length_row_ref,
    home, extra, outgoing, along, lon, lat, field, back,
    in_sem, send_sem, home_sem, extra_sem, back_sem, own_sem, out_sem, column_sem,
):
    mx, my = lax.axis_index("sx"), lax.axis_index("sy")
    me = mx * SY + my
    here = my * SX + mx
    z, y, x, core = mx // 4, mx % 4, my // 2, my % 2

    def partner(step):
        k = DEVICES - step
        px = ((z + (k // 4) % 4) % 4) * 4 + (y + (k // 16) % 4) % 4
        py = ((x + k % 4) % 4) * 2 + (core + k // 64) % 2
        return px, py

    barrier = pltpu.get_barrier_semaphore()

    @pl.loop(1, SX)
    def _(step):
        pl.semaphore_signal(barrier, inc=1, device_id=(lax.rem(mx + step, SX), my), device_id_type=MESH)

    @pl.loop(1, SY)
    def _(step):
        pl.semaphore_signal(barrier, inc=1, device_id=(mx, lax.rem(my + step, SY)), device_id_type=MESH)

    cut = LIFT // 2
    small = []
    for at, (src, dst) in enumerate(
        ((owners_hbm, owners_ref), (vertical_hbm, vertical_ref), (length_hbm, length_ref))
    ):
        small.append(pltpu.make_async_copy(src, dst, in_sem.at[4 + at]))
        small[-1].start()
    loads = []
    for part in range(2):
        rows = pl.ds(part * cut, cut)
        for at, (src, dst) in enumerate(((control_hbm, control), (deviation_hbm, deviation))):
            loads.append(pltpu.make_async_copy(src.at[rows], dst.at[rows], in_sem.at[2 * part + at]))
    for load in loads:
        load.start()

    control[LIFT:, :] = jnp.zeros((ROWS, COLS), jnp.float32)
    deviation[LIFT:, :] = jnp.zeros((ROWS, COLS), jnp.float32)
    length_row_ref[...] = jnp.ones((1, PLACES), jnp.float32)
    matrix[...] = jnp.zeros((PLACES, PLACES), jnp.float32)
    for load in small:
        load.wait()
    for v in range(VARS):
        length_row_ref[:, v * 128 : v * 128 + LEV] = length_ref[v : v + 1, :]
        matrix[v * 128 : v * 128 + LEV, v * 128 : v * 128 + LEV] = vertical_ref[:, v, :]
    slab = lax.broadcasted_iota(jnp.int32, (PLACES, VARS * LEV), 0)
    level = slab % 128
    number = jnp.where(level < LEV, slab - slab // 128, -1)
    listed = lax.broadcasted_iota(jnp.int32, (PLACES, VARS * LEV), 1) == number
    owners = owners_ref[...].astype(jnp.float32)
    owner_col = jnp.sum(jnp.where(listed, owners + 1.0, 0.0), axis=1, keepdims=True) - 1.0
    shape = (PLACES, PLACES)
    down = lax.broadcasted_iota(jnp.int32, shape, 0)
    over = lax.broadcasted_iota(jnp.int32, shape, 1)
    owner_row = jnp.sum(jnp.where(down == over, owner_col, 0.0), axis=0, keepdims=True)
    row = lax.broadcasted_iota(jnp.int32, (PLACES, 1), 0)
    side = jnp.where(row < DEVICES, 1 - core, core)
    label = (4 * ((row % DEVICES) // 2) + 2 * side + row % 2).astype(jnp.float32)
    home_hot, extra_hot, taken_col = where_to(owner_col, owner_row, label)
    high, low = split(matrix[...])

    def lift(hot, first):
        hot = hot.astype(jnp.bfloat16)
        rows = (dot(hot, high).astype(jnp.bfloat16), dot(hot, low).astype(jnp.bfloat16))
        for i in range(0, ROWS, 2):
            lifted = dot3(rows, (scaled[0, i // 2], scaled[1, i // 2]))
            for r in (0, 1):
                at = pl.ds(first * ROWS + i + r, hot.shape[0], stride=ROWS)
                pieces[at, :] = lifted[:, r * COLS : (r + 1) * COLS]

    def seat(px, py, other_core):
        return jnp.where(py % 2 == other_core, DEVICES, 0) + 2 * (px * 4 + py // 2)

    def two(first, px, py):
        return pieces.at[pl.ds((first + seat(px, py, core)) * ROWS, 2 * ROWS)]

    def scatter(first, into, sem, begin, end):
        @pl.loop(begin, end)
        def _(step):
            px, py = partner(step)
            pltpu.make_async_remote_copy(
                src_ref=two(first, px, py),
                dst_ref=into.at[here],
                send_sem=send_sem,
                recv_sem=sem,
                device_id=(px, py),
                device_id_type=MESH,
            ).start()

    pl.semaphore_wait(barrier, SX + SY - 2)

    @pl.loop(1, SY)
    def _(step):
        pl.semaphore_signal(column_sem, inc=1, device_id=(mx, lax.rem(my + step, SY)), device_id_type=MESH)

    for load in loads:
        load.wait()
    for i in range(0, ROWS, 2):
        sides = []
        for r in (i, i + 1):
            halves = []
            for v in range(VARS):
                at = pl.ds(v * LEV * ROWS + r, 128, stride=ROWS)
                halves.append(control[at, :] * deviation[at, :])
            sides.append(jnp.concatenate(halves, axis=0))
        scaled[0, i // 2], scaled[1, i // 2] = split(jnp.concatenate(sides, axis=1))

    lift(home_hot[:DEVICES], 0)
    pl.semaphore_wait(column_sem, SY - 1)
    scatter(0, home, home_sem, 1, DEVICES // 2 + 1)
    lift(home_hot[DEVICES:], DEVICES)
    scatter(0, home, home_sem, DEVICES // 2 + 1, DEVICES)
    own_home = pltpu.make_async_copy(two(0, mx, my), home.at[here], own_sem.at[0])
    own_home.start()
    lift(extra_hot, PLACES)
    scatter(PLACES, extra, extra_sem, 1, DEVICES)
    own_extra = pltpu.make_async_copy(two(PLACES, mx, my), extra.at[here], own_sem.at[1])
    own_extra.start()

    turned_high, turned_low = split(matrix[...].T)
    home_turned = home_hot.T.astype(jnp.bfloat16)
    whole = dot(turned_high, home_turned) + dot(turned_low, home_turned)
    for side in range(2):
        back[side * PLACES : (side + 1) * PLACES, :] = whole[:, side * COLS : (side + 1) * COLS]
    out = [pltpu.make_async_copy(back, returned.at[pl.ds(PLACES * ROWS, 2 * PLACES)], out_sem.at[4])]
    out[0].start()
    length_row = length_row_ref[...]
    owned = []
    for at, hot in ((0, home_hot), (2, extra_hot)):
        used = jnp.sum(hot, axis=1, keepdims=True)
        long = jnp.sum(hot * length_row, axis=1, keepdims=True) + (1.0 - used)
        for h in range(2):
            mine = jnp.where(label == (2 * me + h).astype(jnp.float32), 1.0, 0.0)
            smooth_matrices(jnp.sum(mine * long, axis=0, keepdims=True), lon.at[at + h], lat.at[at + h])
            if at == 0:
                owned.append(jnp.sum(mine * taken_col, axis=0, keepdims=True))

    def smooth(h, source, keep):
        for t in range(4):
            blocks = [
                source[pl.ds((2 * t + b) * SX, SX), h * ROWS : (h + 1) * ROWS].reshape(NLON, COLS) for b in range(2)
            ]
            lifted = split(jnp.concatenate(blocks, axis=1))
            along[:, t * 256 : (t + 1) * 256] = dot3((lon[keep, 0], lon[keep, 1]), lifted)
        for t in range(4):
            begin, end = max(0, 256 * t - 128), min(NLAT, 256 * t + 384)
            taps = pl.ds(begin - (256 * t - 128), end - begin)
            done = dot3(split(along[:, begin:end]), (lat[keep, 0, taps, :], lat[keep, 1, taps, :]))
            if keep < 2:
                field[keep, :, t * 256 : (t + 1) * 256] = done * owned[keep]
                for b in range(2):
                    outgoing[pl.ds((2 * t + b) * SX, SX), h * ROWS : (h + 1) * ROWS] = done[
                        :, b * COLS : (b + 1) * COLS
                    ].reshape(SX, ROWS, COLS)
            else:
                field[keep, :, t * 256 : (t + 1) * 256] = done

    own_home.wait()
    pltpu.make_async_copy(home.at[pl.ds(0, DEVICES - 1)], home.at[pl.ds(0, DEVICES - 1)], home_sem).wait()
    for h in range(2):
        smooth(h, home, h)

    def into(other_core):
        return returned.at[pl.ds(ROWS * seat(mx, my, other_core), 2 * ROWS)]

    own_back = pltpu.make_async_copy(outgoing.at[here], into(core), own_sem.at[2])
    own_back.start()

    @pl.loop(1, DEVICES)
    def _(step):
        px, py = partner(step)
        pltpu.make_async_remote_copy(
            src_ref=outgoing.at[py * SX + px],
            dst_ref=into(py % 2),
            send_sem=send_sem,
            recv_sem=back_sem,
            device_id=(px, py),
            device_id_type=MESH,
        ).start()

    def write(h):
        out.append(pltpu.make_async_copy(field.at[h], field_hbm.at[h], out_sem.at[h]))
        out[-1].start()

    for h in range(2):
        write(h)
    own_extra.wait()
    pltpu.make_async_copy(extra.at[pl.ds(0, DEVICES - 1)], extra.at[pl.ds(0, DEVICES - 1)], extra_sem).wait()
    for h in range(2):
        smooth(h, extra, 2 + h)
        write(2 + h)
    own_back.wait()
    for copy in out:
        copy.wait()
    arrived = returned.at[pl.ds(0, 2 * ROWS * (DEVICES - 1))]
    pltpu.make_async_copy(arrived, arrived, back_sem).wait()
    for _ in range(3):
        pltpu.make_async_copy(arrived, arrived, send_sem).wait()


def settle_kernel(
    returned_hbm, deviation_hbm, field_hbm,
    result_hbm, fields_hbm,
    returned, deviation, back, field, result, in_sem, out_sem,
):
    half = ROWS // 2
    tail = pl.ds(PLACES, 2 * PLACES // ROWS)
    loads = [pltpu.make_async_copy(returned_hbm.at[tail], back, in_sem.at[0])]
    for part in range(2):
        rows = pl.ds(part * half, half)
        at = 1 + 2 * part
        loads.append(pltpu.make_async_copy(returned_hbm.at[pl.ds(0, PLACES), rows], returned.at[part], in_sem.at[at]))
        loads.append(pltpu.make_async_copy(deviation_hbm.at[:, rows], deviation.at[part], in_sem.at[at + 1]))
    slots = [pltpu.make_async_copy(field_hbm.at[h], field.at[h], in_sem.at[5 + h]) for h in range(4)]
    for load in loads + slots:
        load.start()
    out = []

    def write(src, dst):
        out.append(pltpu.make_async_copy(src, dst, out_sem.at[len(out)]))
        out[-1].start()

    loads[0].wait()
    flat = back[...].reshape(2 * PLACES, COLS)
    ways = split(jnp.concatenate([flat[:PLACES], flat[PLACES:]], axis=1))
    for part in range(2):
        for load in loads[1 + 2 * part : 3 + 2 * part]:
            load.wait()
        arrived = returned.at[part].reshape(PLACES * half, COLS)
        spread = deviation.at[part].reshape(VARS * LEV * half, COLS)
        settled_to = result.at[part].reshape(VARS * LEV * half, COLS)
        for i in range(0, half, 2):
            sides = [arrived[pl.ds(i + r, PLACES, stride=half), :] for r in range(2)]
            settled = dot3(ways, split(jnp.concatenate(sides, axis=1)))
            for r in range(2):
                for v in range(VARS):
                    at = pl.ds(v * LEV * half + i + r, LEV, stride=half)
                    settled_to[at, :] = spread[at, :] * settled[v * 128 : v * 128 + LEV, r * COLS : (r + 1) * COLS]
            slot = part * 4 + i // 2 - 2
            if 0 <= slot < 4:
                slots[slot].wait()
                write(field.at[slot], fields_hbm.at[slot])
        write(result.at[part], result_hbm.at[:, pl.ds(part * half, half)])
    for copy in out:
        copy.wait()


def local(control, deviation, vertical, length, owners):
    f32, bf16 = jnp.float32, jnp.bfloat16
    hbm = pl.BlockSpec(memory_space=pl.ANY)
    dma = pltpu.SemaphoreType.DMA
    flat, square = (LIFT, COLS), (PLACES, PLACES)
    block = (DEVICES, 2 * ROWS, COLS)
    deviation = deviation.reshape(flat)
    returned, field = pl.pallas_call(
        travel_kernel,
        out_shape=[
            jax.ShapeDtypeStruct((PLACES * ROWS + 2 * PLACES, COLS), f32),
            jax.ShapeDtypeStruct((4, NLON, NLAT), f32),
        ],
        in_specs=[hbm] * 5,
        out_specs=[hbm] * 2,
        scratch_shapes=[
            pltpu.VMEM((LIFT + ROWS, COLS), f32),
            pltpu.VMEM((LIFT + ROWS, COLS), f32),
            pltpu.VMEM((LEV, VARS, LEV), f32),
            pltpu.VMEM((VARS, LEV), f32),
            pltpu.VMEM((1, VARS * LEV), jnp.int32),
            pltpu.VMEM((2, ROWS // 2, PLACES, 2 * COLS), bf16),
            pltpu.VMEM((2 * PLACES * ROWS, COLS), f32),
            pltpu.VMEM(square, f32),
            pltpu.VMEM((1, PLACES), f32),
            pltpu.VMEM(block, f32),
            pltpu.VMEM(block, f32),
            pltpu.VMEM(block, f32),
            pltpu.VMEM((NLON, NLAT), f32),
            pltpu.VMEM((4, 2, NLON, NLON), bf16),
            pltpu.VMEM((4, 2, 512, 256), bf16),
            pltpu.VMEM((4, NLON, NLAT), f32),
            pltpu.VMEM((2 * PLACES, COLS), f32),
            dma((7,)), dma, dma, dma, dma, dma((3,)), dma((5,)),
            pltpu.SemaphoreType.REGULAR,
        ],
        compiler_params=pltpu.CompilerParams(
            collective_id=0, has_side_effects=True, vmem_limit_bytes=VMEM_LIMIT
        ),
        name="travel",
    )(control.reshape(flat), deviation, vertical.transpose(1, 0, 2), length, owners.reshape(1, VARS * LEV))

    half = (2, VARS * LEV, ROWS // 2, COLS)
    result, fields = pl.pallas_call(
        settle_kernel,
        out_shape=[
            jax.ShapeDtypeStruct((VARS * LEV, ROWS, COLS), f32),
            jax.ShapeDtypeStruct((4, NLON, NLAT), f32),
        ],
        in_specs=[hbm] * 3,
        out_specs=[hbm] * 2,
        scratch_shapes=[
            pltpu.VMEM((2, PLACES, ROWS // 2, COLS), f32),
            pltpu.VMEM(half, f32),
            pltpu.VMEM((2 * PLACES // ROWS, ROWS, COLS), f32),
            pltpu.VMEM((4, NLON, NLAT), f32),
            pltpu.VMEM(half, f32),
            dma((9,)),
            dma((6,)),
        ],
        compiler_params=pltpu.CompilerParams(vmem_limit_bytes=SETTLE_LIMIT),
        name="settle",
    )(
        returned.reshape(PLACES + 2 * PLACES // ROWS, ROWS, COLS),
        deviation.reshape(VARS * LEV, ROWS, COLS),
        field,
    )
    return result.reshape(VARS, LEV, ROWS, COLS), fields.reshape(1, 4, NLON, NLAT)


def solution(mesh):
    return jax.shard_map(
        local,
        mesh=mesh,
        in_specs=(P(None, None, "sx", "sy"), P(None, None, "sx", "sy"), P(), P(), P()),
        out_specs=(P(None, None, "sx", "sy"), P(("sx", "sy"), None, None, None)),
        check_vma=False,
    )
```

```python
import jax
import jax.numpy as jnp
from jax import lax
from jax.experimental import pallas as pl
from jax.experimental.pallas import tpu as pltpu
from jax.sharding import PartitionSpec as P

MESH = pl.DeviceIdType.MESH
BAND = 12
VARS, LEV, ROWS, COLS = 2, 127, 16, 128
SX, SY = 16, 8
DEVICES = SX * SY
VMEM_LIMIT = 57 * 2**20
SETTLE_LIMIT = 103 * 2**19
NLON, NLAT = 256, 1024
PLACES = 2 * DEVICES
LIFT = VARS * LEV * ROWS


def split(x):
    high = x.astype(jnp.bfloat16)
    return high, (x - high.astype(jnp.float32)).astype(jnp.bfloat16)


def dot(a, b):
    return jnp.dot(a, b, preferred_element_type=jnp.float32)


def dot3(a, b):
    return dot(a[0], b[0]) + (dot(a[0], b[1]) + dot(a[1], b[0]))


def where_to(owner_col, owner_row, label):
    shape = (PLACES, PLACES)
    down = lax.broadcasted_iota(jnp.int32, shape, 0).astype(jnp.float32)
    over = lax.broadcasted_iota(jnp.int32, shape, 1).astype(jnp.float32)
    one = lambda c: jnp.where(c, 1.0, 0.0)
    device_col, device_row = jnp.floor(label / 2.0), jnp.floor(over[:1] / 2.0)
    count_col = jnp.sum(one(owner_row == device_col), axis=1, keepdims=True)
    count_row = jnp.sum(one(owner_col == device_row), axis=0, keepdims=True)
    taken_col = one(count_col > label - 2.0 * device_col)
    taken_row = one(count_row > over[:1] - 2.0 * device_row)
    free_rank_col = jnp.sum((1.0 - taken_row) * one(over < label), axis=1, keepdims=True)
    same = one(owner_col == owner_row)
    above = one(down < over)
    slot_row = jnp.sum(same * above, axis=0, keepdims=True)
    slot_col = jnp.sum(same * one(over < down), axis=1, keepdims=True)
    extra_row = one(owner_row >= 0.0) * one(slot_row >= 2.0)
    extra_col = one(owner_col >= 0.0) * one(slot_col >= 2.0)
    place_row = 2.0 * owner_row + slot_row
    rank_row = jnp.sum(extra_col * above, axis=0, keepdims=True)
    native = one(label == jnp.where(owner_row >= 0.0, place_row, -1.0)) * (1.0 - extra_row)
    lent = one(free_rank_col == rank_row) * extra_row * (1.0 - taken_col)
    extra = one(label == place_row - 2.0) * extra_row
    return native + lent, extra, taken_col


def smooth_matrices(long, lon, lat):
    lane = lax.broadcasted_iota(jnp.int32, (8, COLS), 1)
    offset = (lane - BAND).astype(jnp.float32)
    bell = jnp.where(lane <= 2 * BAND, jnp.exp(-(offset * offset) / (2.0 * long * long)), 0.0)
    norm = jnp.sqrt(jnp.sum(bell * bell, axis=1, keepdims=True))[0:1, :]

    def weigh(d):
        near = (d >= -BAND) & (d <= BAND)
        d = d.astype(jnp.float32)
        return jnp.where(near, jnp.exp(-(d * d) / (2.0 * long * long)) / norm, 0.0)

    shape = (NLON, NLON)
    d = lax.broadcasted_iota(jnp.int32, shape, 1) - lax.broadcasted_iota(jnp.int32, shape, 0)
    d = jnp.where(d >= NLON // 2, d - NLON, jnp.where(d < -(NLON // 2), d + NLON, d))
    lon[0], lon[1] = split(weigh(d))
    shape = (512, 256)
    d = lax.broadcasted_iota(jnp.int32, shape, 0) - 128 - lax.broadcasted_iota(jnp.int32, shape, 1)
    lat[0], lat[1] = split(weigh(d))


def travel_kernel(
    control_hbm, deviation_hbm, vertical_hbm, length_hbm, owners_hbm,
    returned, field_hbm,
    control, deviation, vertical_ref, length_ref, owners_ref, scaled, pieces, matrix, length_row_ref,
    home, extra, outgoing, along, lon, lat, field, back,
    in_sem, send_sem, home_sem, extra_sem, back_sem, own_sem, out_sem, column_sem,
):
    mx, my = lax.axis_index("sx"), lax.axis_index("sy")
    me = mx * SY + my
    here = my * SX + mx
    z, y, x, core = mx // 4, mx % 4, my // 2, my % 2

    def partner(step):
        k = DEVICES - step
        px = ((z + k // 16 + k // 4) % 4) * 4 + (y + k // 4) % 4
        py = ((x + k % 4) % 4) * 2 + (core + k // 64) % 2
        return px, py

    barrier = pltpu.get_barrier_semaphore()

    @pl.loop(1, SX)
    def _(step):
        pl.semaphore_signal(barrier, inc=1, device_id=(lax.rem(mx + step, SX), my), device_id_type=MESH)

    @pl.loop(1, SY)
    def _(step):
        pl.semaphore_signal(barrier, inc=1, device_id=(mx, lax.rem(my + step, SY)), device_id_type=MESH)

    cut = LIFT // 2
    small = []
    for at, (src, dst) in enumerate(
        ((owners_hbm, owners_ref), (vertical_hbm, vertical_ref), (length_hbm, length_ref))
    ):
        small.append(pltpu.make_async_copy(src, dst, in_sem.at[4 + at]))
        small[-1].start()
    loads = []
    for part in range(2):
        rows = pl.ds(part * cut, cut)
        for at, (src, dst) in enumerate(((control_hbm, control), (deviation_hbm, deviation))):
            loads.append(pltpu.make_async_copy(src.at[rows], dst.at[rows], in_sem.at[2 * part + at]))
    for load in loads:
        load.start()

    control[LIFT:, :] = jnp.zeros((ROWS, COLS), jnp.float32)
    deviation[LIFT:, :] = jnp.zeros((ROWS, COLS), jnp.float32)
    length_row_ref[...] = jnp.ones((1, PLACES), jnp.float32)
    matrix[...] = jnp.zeros((PLACES, PLACES), jnp.float32)
    for load in small:
        load.wait()
    for v in range(VARS):
        length_row_ref[:, v * 128 : v * 128 + LEV] = length_ref[v : v + 1, :]
        matrix[v * 128 : v * 128 + LEV, v * 128 : v * 128 + LEV] = vertical_ref[:, v, :]
    slab = lax.broadcasted_iota(jnp.int32, (PLACES, VARS * LEV), 0)
    level = slab % 128
    number = jnp.where(level < LEV, slab - slab // 128, -1)
    listed = lax.broadcasted_iota(jnp.int32, (PLACES, VARS * LEV), 1) == number
    owners = owners_ref[...].astype(jnp.float32)
    owner_col = jnp.sum(jnp.where(listed, owners + 1.0, 0.0), axis=1, keepdims=True) - 1.0
    shape = (PLACES, PLACES)
    down = lax.broadcasted_iota(jnp.int32, shape, 0)
    over = lax.broadcasted_iota(jnp.int32, shape, 1)
    owner_row = jnp.sum(jnp.where(down == over, owner_col, 0.0), axis=0, keepdims=True)
    row = lax.broadcasted_iota(jnp.int32, (PLACES, 1), 0)
    side = jnp.where(row < DEVICES, 1 - core, core)
    label = (4 * ((row % DEVICES) // 2) + 2 * side + row % 2).astype(jnp.float32)
    home_hot, extra_hot, taken_col = where_to(owner_col, owner_row, label)
    high, low = split(matrix[...])

    def lift(hot, first):
        hot = hot.astype(jnp.bfloat16)
        rows = (dot(hot, high).astype(jnp.bfloat16), dot(hot, low).astype(jnp.bfloat16))
        for i in range(0, ROWS, 2):
            lifted = dot3(rows, (scaled[0, i // 2], scaled[1, i // 2]))
            for r in (0, 1):
                at = pl.ds(first * ROWS + i + r, hot.shape[0], stride=ROWS)
                pieces[at, :] = lifted[:, r * COLS : (r + 1) * COLS]

    def seat(px, py, other_core):
        return jnp.where(py % 2 == other_core, DEVICES, 0) + 2 * (px * 4 + py // 2)

    def two(first, px, py):
        return pieces.at[pl.ds((first + seat(px, py, core)) * ROWS, 2 * ROWS)]

    def scatter(first, into, sem, begin, end):
        @pl.loop(begin, end)
        def _(step):
            px, py = partner(step)
            pltpu.make_async_remote_copy(
                src_ref=two(first, px, py),
                dst_ref=into.at[here],
                send_sem=send_sem,
                recv_sem=sem,
                device_id=(px, py),
                device_id_type=MESH,
            ).start()

    pl.semaphore_wait(barrier, SX + SY - 2)

    @pl.loop(1, SY)
    def _(step):
        pl.semaphore_signal(column_sem, inc=1, device_id=(mx, lax.rem(my + step, SY)), device_id_type=MESH)

    for load in loads:
        load.wait()
    for i in range(0, ROWS, 2):
        sides = []
        for r in (i, i + 1):
            halves = []
            for v in range(VARS):
                at = pl.ds(v * LEV * ROWS + r, 128, stride=ROWS)
                halves.append(control[at, :] * deviation[at, :])
            sides.append(jnp.concatenate(halves, axis=0))
        scaled[0, i // 2], scaled[1, i // 2] = split(jnp.concatenate(sides, axis=1))

    lift(home_hot[:DEVICES], 0)
    pl.semaphore_wait(column_sem, SY - 1)
    scatter(0, home, home_sem, 1, DEVICES // 2 + 1)
    lift(home_hot[DEVICES:], DEVICES)
    scatter(0, home, home_sem, DEVICES // 2 + 1, DEVICES)
    own_home = pltpu.make_async_copy(two(0, mx, my), home.at[here], own_sem.at[0])
    own_home.start()
    lift(extra_hot, PLACES)
    scatter(PLACES, extra, extra_sem, 1, DEVICES)
    own_extra = pltpu.make_async_copy(two(PLACES, mx, my), extra.at[here], own_sem.at[1])
    own_extra.start()

    turned_high, turned_low = split(matrix[...].T)
    home_turned = home_hot.T.astype(jnp.bfloat16)
    whole = dot(turned_high, home_turned) + dot(turned_low, home_turned)
    for side in range(2):
        back[side * PLACES : (side + 1) * PLACES, :] = whole[:, side * COLS : (side + 1) * COLS]
    out = [pltpu.make_async_copy(back, returned.at[pl.ds(PLACES * ROWS, 2 * PLACES)], out_sem.at[4])]
    out[0].start()
    length_row = length_row_ref[...]
    owned = []
    for at, hot in ((0, home_hot), (2, extra_hot)):
        used = jnp.sum(hot, axis=1, keepdims=True)
        long = jnp.sum(hot * length_row, axis=1, keepdims=True) + (1.0 - used)
        for h in range(2):
            mine = jnp.where(label == (2 * me + h).astype(jnp.float32), 1.0, 0.0)
            smooth_matrices(jnp.sum(mine * long, axis=0, keepdims=True), lon.at[at + h], lat.at[at + h])
            if at == 0:
                owned.append(jnp.sum(mine * taken_col, axis=0, keepdims=True))

    def smooth(h, source, keep):
        for t in range(4):
            blocks = [
                source[pl.ds((2 * t + b) * SX, SX), h * ROWS : (h + 1) * ROWS].reshape(NLON, COLS) for b in range(2)
            ]
            lifted = split(jnp.concatenate(blocks, axis=1))
            along[:, t * 256 : (t + 1) * 256] = dot3((lon[keep, 0], lon[keep, 1]), lifted)
        for t in range(4):
            begin, end = max(0, 256 * t - 128), min(NLAT, 256 * t + 384)
            taps = pl.ds(begin - (256 * t - 128), end - begin)
            done = dot3(split(along[:, begin:end]), (lat[keep, 0, taps, :], lat[keep, 1, taps, :]))
            if keep < 2:
                field[keep, :, t * 256 : (t + 1) * 256] = done * owned[keep]
                for b in range(2):
                    outgoing[pl.ds((2 * t + b) * SX, SX), h * ROWS : (h + 1) * ROWS] = done[
                        :, b * COLS : (b + 1) * COLS
                    ].reshape(SX, ROWS, COLS)
            else:
                field[keep, :, t * 256 : (t + 1) * 256] = done

    own_home.wait()
    pltpu.make_async_copy(home.at[pl.ds(0, DEVICES - 1)], home.at[pl.ds(0, DEVICES - 1)], home_sem).wait()
    for h in range(2):
        smooth(h, home, h)

    def into(other_core):
        return returned.at[pl.ds(ROWS * seat(mx, my, other_core), 2 * ROWS)]

    own_back = pltpu.make_async_copy(outgoing.at[here], into(core), own_sem.at[2])
    own_back.start()

    @pl.loop(1, DEVICES)
    def _(step):
        px, py = partner(step)
        pltpu.make_async_remote_copy(
            src_ref=outgoing.at[py * SX + px],
            dst_ref=into(py % 2),
            send_sem=send_sem,
            recv_sem=back_sem,
            device_id=(px, py),
            device_id_type=MESH,
        ).start()

    def write(h):
        out.append(pltpu.make_async_copy(field.at[h], field_hbm.at[h], out_sem.at[h]))
        out[-1].start()

    for h in range(2):
        write(h)
    own_extra.wait()
    pltpu.make_async_copy(extra.at[pl.ds(0, DEVICES - 1)], extra.at[pl.ds(0, DEVICES - 1)], extra_sem).wait()
    for h in range(2):
        smooth(h, extra, 2 + h)
        write(2 + h)
    own_back.wait()
    for copy in out:
        copy.wait()
    arrived = returned.at[pl.ds(0, 2 * ROWS * (DEVICES - 1))]
    pltpu.make_async_copy(arrived, arrived, back_sem).wait()
    for _ in range(3):
        pltpu.make_async_copy(arrived, arrived, send_sem).wait()


def settle_kernel(
    returned_hbm, deviation_hbm, field_hbm,
    result_hbm, fields_hbm,
    returned, deviation, back, field, result, in_sem, out_sem,
):
    half = ROWS // 2
    tail = pl.ds(PLACES, 2 * PLACES // ROWS)
    loads = [pltpu.make_async_copy(returned_hbm.at[tail], back, in_sem.at[0])]
    for part in range(2):
        rows = pl.ds(part * half, half)
        at = 1 + 2 * part
        loads.append(pltpu.make_async_copy(returned_hbm.at[pl.ds(0, PLACES), rows], returned.at[part], in_sem.at[at]))
        loads.append(pltpu.make_async_copy(deviation_hbm.at[:, rows], deviation.at[part], in_sem.at[at + 1]))
    slots = [pltpu.make_async_copy(field_hbm.at[h], field.at[h], in_sem.at[5 + h]) for h in range(4)]
    for load in loads + slots:
        load.start()
    out = []

    def write(src, dst):
        out.append(pltpu.make_async_copy(src, dst, out_sem.at[len(out)]))
        out[-1].start()

    loads[0].wait()
    flat = back[...].reshape(2 * PLACES, COLS)
    ways = split(jnp.concatenate([flat[:PLACES], flat[PLACES:]], axis=1))
    for part in range(2):
        for load in loads[1 + 2 * part : 3 + 2 * part]:
            load.wait()
        arrived = returned.at[part].reshape(PLACES * half, COLS)
        spread = deviation.at[part].reshape(VARS * LEV * half, COLS)
        settled_to = result.at[part].reshape(VARS * LEV * half, COLS)
        for i in range(0, half, 2):
            sides = [arrived[pl.ds(i + r, PLACES, stride=half), :] for r in range(2)]
            settled = dot3(ways, split(jnp.concatenate(sides, axis=1)))
            for r in range(2):
                for v in range(VARS):
                    at = pl.ds(v * LEV * half + i + r, LEV, stride=half)
                    settled_to[at, :] = spread[at, :] * settled[v * 128 : v * 128 + LEV, r * COLS : (r + 1) * COLS]
            slot = part * 4 + i // 2 - 2
            if 0 <= slot < 4:
                slots[slot].wait()
                write(field.at[slot], fields_hbm.at[slot])
        write(result.at[part], result_hbm.at[:, pl.ds(part * half, half)])
    for copy in out:
        copy.wait()


def local(control, deviation, vertical, length, owners):
    f32, bf16 = jnp.float32, jnp.bfloat16
    hbm = pl.BlockSpec(memory_space=pl.ANY)
    dma = pltpu.SemaphoreType.DMA
    flat, square = (LIFT, COLS), (PLACES, PLACES)
    block = (DEVICES, 2 * ROWS, COLS)
    deviation = deviation.reshape(flat)
    returned, field = pl.pallas_call(
        travel_kernel,
        out_shape=[
            jax.ShapeDtypeStruct((PLACES * ROWS + 2 * PLACES, COLS), f32),
            jax.ShapeDtypeStruct((4, NLON, NLAT), f32),
        ],
        in_specs=[hbm] * 5,
        out_specs=[hbm] * 2,
        scratch_shapes=[
            pltpu.VMEM((LIFT + ROWS, COLS), f32),
            pltpu.VMEM((LIFT + ROWS, COLS), f32),
            pltpu.VMEM((LEV, VARS, LEV), f32),
            pltpu.VMEM((VARS, LEV), f32),
            pltpu.VMEM((1, VARS * LEV), jnp.int32),
            pltpu.VMEM((2, ROWS // 2, PLACES, 2 * COLS), bf16),
            pltpu.VMEM((2 * PLACES * ROWS, COLS), f32),
            pltpu.VMEM(square, f32),
            pltpu.VMEM((1, PLACES), f32),
            pltpu.VMEM(block, f32),
            pltpu.VMEM(block, f32),
            pltpu.VMEM(block, f32),
            pltpu.VMEM((NLON, NLAT), f32),
            pltpu.VMEM((4, 2, NLON, NLON), bf16),
            pltpu.VMEM((4, 2, 512, 256), bf16),
            pltpu.VMEM((4, NLON, NLAT), f32),
            pltpu.VMEM((2 * PLACES, COLS), f32),
            dma((7,)), dma, dma, dma, dma, dma((3,)), dma((5,)),
            pltpu.SemaphoreType.REGULAR,
        ],
        compiler_params=pltpu.CompilerParams(
            collective_id=0, has_side_effects=True, vmem_limit_bytes=VMEM_LIMIT
        ),
        name="travel",
    )(control.reshape(flat), deviation, vertical.transpose(1, 0, 2), length, owners.reshape(1, VARS * LEV))

    half = (2, VARS * LEV, ROWS // 2, COLS)
    result, fields = pl.pallas_call(
        settle_kernel,
        out_shape=[
            jax.ShapeDtypeStruct((VARS * LEV, ROWS, COLS), f32),
            jax.ShapeDtypeStruct((4, NLON, NLAT), f32),
        ],
        in_specs=[hbm] * 3,
        out_specs=[hbm] * 2,
        scratch_shapes=[
            pltpu.VMEM((2, PLACES, ROWS // 2, COLS), f32),
            pltpu.VMEM(half, f32),
            pltpu.VMEM((2 * PLACES // ROWS, ROWS, COLS), f32),
            pltpu.VMEM((4, NLON, NLAT), f32),
            pltpu.VMEM(half, f32),
            dma((9,)),
            dma((6,)),
        ],
        compiler_params=pltpu.CompilerParams(vmem_limit_bytes=SETTLE_LIMIT),
        name="settle",
    )(
        returned.reshape(PLACES + 2 * PLACES // ROWS, ROWS, COLS),
        deviation.reshape(VARS * LEV, ROWS, COLS),
        field,
    )
    return result.reshape(VARS, LEV, ROWS, COLS), fields.reshape(1, 4, NLON, NLAT)


def solution(mesh):
    return jax.shard_map(
        local,
        mesh=mesh,
        in_specs=(P(None, None, "sx", "sy"), P(None, None, "sx", "sy"), P(), P(), P()),
        out_specs=(P(None, None, "sx", "sy"), P(("sx", "sy"), None, None, None)),
        check_vma=False,
    )
```
